256 devices in a mesh: wide: 64 (over x, z, core), narrow: 4 (over y).
Axes of the slice: x: 4, y: 4, z: 8, core: 2. Of those that a mesh axis runs over, the one named last changes fastest.
Arguments:
- node_features: bfloat16 [393216, 128], P(('wide', 'narrow')), may hold values from -6 to 6
- fine_neighbors: int32 [393216, 8], P(('wide', 'narrow')), may hold values from 0 to 2304, as said below
- send_rows: int32 [256, 4, 192], P(('wide', 'narrow')), may hold values from 0 to 1535
- coarse_neighbors: int32 [98304, 8], P(('wide', 'narrow')), may hold values from 0 to 1920, as said below
- coarsest_neighbors: int32 [24576, 8], P(('wide', 'narrow')), may hold values from 0 to 672, as said below
- fine_assign: int32 [393216], P(('wide', 'narrow')), may hold values from 0 to 383, as said below
- coarse_assign: int32 [98304], P(('wide', 'narrow')), may hold values from 0 to 95, as said below
- edge_weights: bfloat16 [3, 3, 128, 128], replicated, may hold values from -0.5 to 0.5
- node_weights: bfloat16 [3, 3, 128, 128], replicated, may hold values from -0.5 to 0.5
- biases: float32 [3, 4, 128], replicated, may hold values from -3 to 3
- gains: float32 [3, 2, 128], replicated, may hold values from 0.1 to 1.9
Outputs:
- fine_output: bfloat16 [393216, 128], P(('wide', 'narrow'))
The draws below stay inside these ranges and needn't reach their ends.
Inputs may be any that keep to these rules, and one draw needn't show every extreme that they name: `fine_neighbors`: values index the partition's fine table; the last row marks an empty slot; no slot names a block whose neighbouring partition does not exist. `coarse_neighbors`: the last row marks an empty slot; every node has 3 or more filled slots. `coarsest_neighbors`: the last row marks an empty slot; every node has 3 or more filled slots. `fine_assign`: within each partition every first coarse node receives exactly 4 fine nodes. `coarse_assign`: within each partition every second coarse node receives exactly 4 first coarse nodes.
All inputs are finite; a program needn't handle non-finite values.
Results may differ from the reference program's by a relative error of at most 0.012.
Values may be sent and summed in bfloat16 or wider, within the bound.
No kernel may reach another device: no remote copies, remote signals or barrier semaphores. Data moves between devices by JAX's collectives and lax.ppermute only.
A program may use at most 64 MiB of HBM per device.

```python
import jax
import jax.numpy as jnp
import numpy as np
from jax import lax

LATENT = 128
EDGE_SLOTS = 8
NODES_DEV = 1536
HALO_ROWS = 192
COARSE_DEV = 384
COARSEST_DEV = 96
WIDE_BITS = 6
NODES = 393216
COARSE_NODES = 98304
COARSEST_NODES = 24576
FINE_TABLE = 2305
COARSE_TABLE = 1921
COARSEST_TABLE = 673
N_WIDE = 64
N_NARROW = 4
DEVICES = 256


def neighbor_helper(key_in, row_total, slot_count, table_size):
    key_one, key_two = jax.random.split(key_in)
    degree = jax.random.randint(key_one, (row_total, 1), 3, slot_count + 1)
    target = jax.random.randint(key_two, (row_total, slot_count), 0, table_size - 1)
    slot_ids = jnp.arange(slot_count)[None, :]
    return (target, slot_ids < degree)


def draw_fine_neighbors(key, part):
    key = jax.random.fold_in(key, 11)
    target, filled = neighbor_helper(key, NODES, EDGE_SLOTS, FINE_TABLE)
    device = jnp.arange(NODES) // NODES_DEV
    wide_pos = (device // N_NARROW)[:, None]
    narrow_pos = (device % N_NARROW)[:, None]
    block = jnp.where(target < NODES_DEV, 0, 1 + (target - NODES_DEV) // HALO_ROWS)
    absent = jnp.logical_or(jnp.logical_and(block == 1, wide_pos == 0), jnp.logical_and(block == 2, wide_pos == N_WIDE - 1))
    absent = jnp.logical_or(absent, jnp.logical_and(block == 3, narrow_pos == 0))
    absent = jnp.logical_or(absent, jnp.logical_and(block == 4, narrow_pos == N_NARROW - 1))
    keep = jnp.logical_and(filled, jnp.logical_not(absent))
    return jnp.where(keep, target, FINE_TABLE - 1).astype(jnp.int32)


def draw_coarse_neighbors(key, part):
    key = jax.random.fold_in(key, 12)
    target, filled = neighbor_helper(key, COARSE_NODES, EDGE_SLOTS, COARSE_TABLE)
    return jnp.where(filled, target, COARSE_TABLE - 1).astype(jnp.int32)


def draw_coarsest_neighbors(key, part):
    key = jax.random.fold_in(key, 13)
    target, filled = neighbor_helper(key, COARSEST_NODES, EDGE_SLOTS, COARSEST_TABLE)
    return jnp.where(filled, target, COARSEST_TABLE - 1).astype(jnp.int32)


def balanced_groups(key_in, row_count, group_count):
    device_keys = jax.random.split(key_in, DEVICES)

    def one_device(device_key):
        return jax.random.permutation(device_key, row_count) % group_count
    return jax.vmap(one_device)(device_keys).reshape(-1).astype(jnp.int32)


def draw_fine_assign(key, part):
    key = jax.random.fold_in(key, 14)
    return balanced_groups(key, NODES_DEV, COARSE_DEV)


def draw_coarse_assign(key, part):
    key = jax.random.fold_in(key, 15)
    return balanced_groups(key, COARSE_DEV, COARSEST_DEV)


def place_ends(values, own_key, smallest, high):
    index_at = [jax.random.randint(jax.random.fold_in(own_key, axis), (), 0, length) for axis, length in enumerate(values.shape)]
    main_axis = values.shape.index(max(values.shape))
    neighbour = index_at[:main_axis] + [(index_at[main_axis] + 1) % values.shape[main_axis]] + index_at[main_axis + 1:]
    return values.at[tuple(index_at)].set(smallest).at[tuple(neighbour)].set(high)


def block_scale(rng, extent, cuts, smallest, top_value):
    def one(dim, parts):
        heights = jax.random.uniform(jax.random.fold_in(jax.random.fold_in(rng, 6), dim), (parts,), jnp.float32, smallest / len(cuts), top_value / len(cuts))
        return jnp.repeat(jnp.exp(heights), extent[dim] // parts).reshape((-1,) + (1,) * (len(extent) - dim - 1))

    factor_of = one(*cuts[0])
    for cut in cuts[1:]:
        factor_of = factor_of * one(*cut)
    return factor_of


def normal_values(own_key, dims, spread, most, cuts=(), held_as=jnp.bfloat16):
    gain = block_scale(own_key, dims, cuts, -0.22, 0.18) if cuts else 1.0
    values = jax.random.normal(own_key, dims, jnp.float32) * spread * gain
    return jnp.minimum(jnp.maximum(values, -most), most).astype(held_as)


def setup_inputs(seed: int = 0) -> dict:
    streams_of = jax.random.split(jax.random.key(seed), 12)
    node_features = normal_values(streams_of[0], (NODES, LATENT), 1.0, 6.0, ((0, 256),))
    fine_neighbors = draw_fine_neighbors(jax.random.fold_in(streams_of[11], 71), 0)
    send_rows = place_ends(jax.random.randint(streams_of[2], (DEVICES, 4, HALO_ROWS), 0, NODES_DEV), jax.random.fold_in(streams_of[2], 1), 0, NODES_DEV - 1).astype(jnp.int32)
    coarse_neighbors = draw_coarse_neighbors(jax.random.fold_in(streams_of[11], 71), 0)
    coarsest_neighbors = draw_coarsest_neighbors(jax.random.fold_in(streams_of[11], 71), 0)
    fine_assign = draw_fine_assign(jax.random.fold_in(streams_of[11], 71), 0)
    coarse_assign = draw_coarse_assign(jax.random.fold_in(streams_of[11], 71), 0)
    edge_weights = normal_values(streams_of[7], (3, 3, LATENT, LATENT), LATENT ** -0.5, 0.5)
    node_weights = normal_values(streams_of[8], (3, 3, LATENT, LATENT), LATENT ** -0.5, 0.5)
    biases = normal_values(streams_of[9], (3, 4, LATENT), 0.5, 3.0, (), jnp.float32)
    gains = jnp.clip(1.0 + 0.18 * jax.random.normal(streams_of[10], (3, 2, LATENT), jnp.float32), 0.1, 1.9)
    return dict(node_features=node_features, fine_neighbors=fine_neighbors, send_rows=send_rows, coarse_neighbors=coarse_neighbors, coarsest_neighbors=coarsest_neighbors, fine_assign=fine_assign, coarse_assign=coarse_assign, edge_weights=edge_weights, node_weights=node_weights, biases=biases, gains=gains)


def layer_norm(values, gain_row):
    row_mean = lax.optimization_barrier(jnp.mean(values, axis=-1, keepdims=True))
    centred = values - row_mean
    row_var = lax.optimization_barrier(jnp.mean(centred * centred, axis=-1, keepdims=True))
    return centred * lax.rsqrt(row_var + 1e-05) * gain_row

def level_step(local_rows, lookup, neighbors, edge_mats, node_mats, bias_rows, gain_rows):
    row_count, slot_count = neighbors.shape
    receive = jnp.dot(local_rows, edge_mats[0], preferred_element_type=jnp.float32) + bias_rows[0]
    sender = jnp.dot(lookup, edge_mats[1], preferred_element_type=jnp.float32)
    picked = jnp.take(sender, neighbors.reshape(-1), axis=0).reshape(row_count, slot_count, -1)
    hidden = jax.nn.relu(receive[:, None, :] + picked).astype(jnp.bfloat16)
    message = jnp.dot(hidden.reshape(row_count * slot_count, -1), edge_mats[2], preferred_element_type=jnp.float32) + bias_rows[1]
    message = layer_norm(message, gain_rows[0]).reshape(row_count, slot_count, -1)
    usable = neighbors < lookup.shape[0] - 1
    summed = lax.optimization_barrier(jnp.sum(jnp.where(usable[:, :, None], message, jnp.float32(0.0)), axis=1)).astype(jnp.bfloat16)
    update = jnp.dot(local_rows, node_mats[0], preferred_element_type=jnp.float32)
    update = update + jnp.dot(summed, node_mats[1], preferred_element_type=jnp.float32) + bias_rows[2]
    update = jax.nn.relu(update).astype(jnp.bfloat16)
    output = layer_norm(jnp.dot(update, node_mats[2], preferred_element_type=jnp.float32) + bias_rows[3], gain_rows[1])
    return (local_rows.astype(jnp.float32) + output).astype(jnp.bfloat16)

def pool_rows(local_rows, assignment, group_count):
    summed = jax.ops.segment_sum(local_rows.astype(jnp.float32), assignment, num_segments=group_count)
    return (summed * 0.25).astype(jnp.bfloat16)

def unpool_rows(local_rows, coarse, assignment):
    return (local_rows.astype(jnp.float32) + jnp.take(coarse, assignment, axis=0).astype(jnp.float32)).astype(jnp.bfloat16)

def run_level(local_rows, lookup, neighbors, edge_mats, node_mats, bias_rows, gain_rows):

    def one_column(pieces):
        return jax.vmap(level_step, in_axes=(0, 0, 0, None, None, None, None))(pieces[0], pieces[1], pieces[2], edge_mats, node_mats, bias_rows, gain_rows)
    return lax.map(one_column, (local_rows, lookup, neighbors))

def reference(node_features, fine_neighbors, send_rows, coarse_neighbors, coarsest_neighbors, fine_assign, coarse_assign, edge_weights, node_weights, biases, gains):
    wide_count = N_WIDE
    narrow_count = N_NARROW
    features = node_features.reshape(wide_count, narrow_count, NODES_DEV, LATENT)
    listed = send_rows.reshape(wide_count, narrow_count, 4, HALO_ROWS)

    def pick_rows(block_rows, block_list):
        return jnp.take(block_rows, block_list.reshape(-1), axis=0).reshape(4, HALO_ROWS, LATENT)
    outgoing = jax.vmap(jax.vmap(pick_rows))(features, listed)
    zero_wide = jnp.zeros((1, narrow_count, HALO_ROWS, LATENT), jnp.bfloat16)
    zero_narrow = jnp.zeros((wide_count, 1, HALO_ROWS, LATENT), jnp.bfloat16)
    from_low_wide = jnp.concatenate([zero_wide, outgoing[:-1, :, 0]], axis=0)
    from_high_wide = jnp.concatenate([outgoing[1:, :, 1], zero_wide], axis=0)
    from_low_narrow = jnp.concatenate([zero_narrow, outgoing[:, :-1, 2]], axis=1)
    from_high_narrow = jnp.concatenate([outgoing[:, 1:, 3], zero_narrow], axis=1)
    blank_row = jnp.zeros((wide_count, narrow_count, 1, LATENT), jnp.bfloat16)
    lookup = jnp.concatenate([features, from_low_wide, from_high_wide, from_low_narrow, from_high_narrow, blank_row], axis=2)
    fine_mid = run_level(features, lookup, fine_neighbors.reshape(wide_count, narrow_count, NODES_DEV, EDGE_SLOTS), edge_weights[0], node_weights[0], biases[0], gains[0])
    assign_fine = fine_assign.reshape(wide_count, narrow_count, NODES_DEV)
    pool_coarse = functools_pool(COARSE_DEV)
    coarse_in = jax.vmap(jax.vmap(pool_coarse))(fine_mid, assign_fine)
    wide_ids = np.arange(wide_count)
    narrow_ids = np.arange(narrow_count)
    lookup = jnp.concatenate([coarse_in, coarse_in[wide_ids ^ 1], coarse_in[wide_ids ^ 2], coarse_in[:, narrow_ids ^ 1], coarse_in[:, narrow_ids ^ 2], blank_row], axis=2)
    coarse_mid = run_level(coarse_in, lookup, coarse_neighbors.reshape(wide_count, narrow_count, COARSE_DEV, EDGE_SLOTS), edge_weights[1], node_weights[1], biases[1], gains[1])
    assign_coarse = coarse_assign.reshape(wide_count, narrow_count, COARSE_DEV)
    pool_coarsest = functools_pool(COARSEST_DEV)
    coarsest_in = jax.vmap(jax.vmap(pool_coarsest))(coarse_mid, assign_coarse)
    pieces = [coarsest_in] + [coarsest_in[wide_ids ^ 1 << bit_number] for bit_number in range(WIDE_BITS)] + [blank_row]
    lookup = jnp.concatenate(pieces, axis=2)
    coarsest_out = run_level(coarsest_in, lookup, coarsest_neighbors.reshape(wide_count, narrow_count, COARSEST_DEV, EDGE_SLOTS), edge_weights[2], node_weights[2], biases[2], gains[2])
    coarse_out = jax.vmap(jax.vmap(unpool_rows))(coarse_mid, coarsest_out, assign_coarse)
    fine_out = jax.vmap(jax.vmap(unpool_rows))(fine_mid, coarse_out, assign_fine)
    return fine_out.reshape(NODES, LATENT)

def functools_pool(group_count):

    def pool_fixed(local_rows, assignment):
        return pool_rows(local_rows, assignment, group_count)
    return pool_fixed
```

```python
import functools

import jax
import jax.numpy as jnp
from jax import lax
from jax.experimental import pallas as pl
from jax.experimental.pallas import tpu as pltpu
from jax.sharding import PartitionSpec as P

F32 = jnp.float32
BF16 = jnp.bfloat16
VMEM_BYTES = 48 * 1024 * 1024


def ring_shift(value, axis, steps):
    count = lax.axis_size(axis)
    return lax.ppermute(value, axis, [(i, (i + steps) % count) for i in range(count)])


def from_partner(block, axis, apart):
    count = lax.axis_size(axis)
    return lax.ppermute(block, axis, [(i, i ^ (1 << apart)) for i in range(count)])


def dot(a, b):
    return jnp.dot(a, b, preferred_element_type=F32)


def one_hot(column, width):
    lanes = lax.broadcasted_iota(jnp.int32, (column.shape[0], width), 1)
    return (column == lanes).astype(BF16)


def centred_columns(matrix):
    wide = matrix.astype(F32)
    return wide - jnp.mean(wide, axis=-1, keepdims=True)


def block_diag(matrix):
    zero = jnp.zeros_like(matrix)
    return jnp.concatenate(
        [jnp.concatenate([matrix, zero], axis=1), jnp.concatenate([zero, matrix], axis=1)], axis=0
    )


def fill_table(table, pieces):
    half = table.shape[0]
    start = 0
    for piece in pieces:
        rows = piece.shape[0]
        cut = min(rows, max(0, half - start))
        if cut > 0:
            table[start : start + cut, 0:128] = piece[0:cut]
        if cut < rows:
            low = start + cut - half
            table[low : low + rows - cut, 128:256] = piece[cut:rows]
        start += rows


def level_block(x, nbr, table, blank, mats, rows):
    w_recv, w_out2, ones2, w_node, w_last, ones1 = mats
    b_hid, b_out2, gain_e, b_node, b_last, gain_n = rows
    half = table.shape[0]
    block = x.shape[0]
    slots = nbr.shape[0]
    receive = dot(x, w_recv) + b_hid
    ids = nbr.T
    total = jnp.zeros((block, 128), F32)
    for k in range(0, slots, 2):
        cols = jnp.concatenate([ids[:, k : k + 1], ids[:, k + 1 : k + 2]], axis=0)
        high = cols >= half
        low = jnp.where(high, cols - half, cols)
        got = dot(one_hot(low, half), table[...])
        sent = jnp.where(high, got[:, 128:256], got[:, 0:128])
        hid = jnp.maximum(jnp.concatenate([receive, receive], axis=0) + sent, 0.0).astype(BF16)
        pair = jnp.concatenate([hid[:block], hid[block:]], axis=1)
        c = dot(pair, w_out2) + b_out2
        var = dot((c * c).astype(BF16), ones2)
        m = c * lax.rsqrt(var + 1e-5)
        first, second = cols[:block] < blank, cols[block:] < blank
        total = total + jnp.where(first, m[:, 0:128], 0.0) + jnp.where(second, m[:, 128:256], 0.0)
    summed = (total * gain_e).astype(BF16)
    upd = jnp.maximum(dot(jnp.concatenate([x, summed], axis=1), w_node) + b_node, 0.0).astype(BF16)
    c = dot(upd, w_last) + b_last
    var = dot((c * c).astype(BF16), ones1)
    return x.astype(F32) + c * lax.rsqrt(var + 1e-5) * gain_n


def level_params(ew, nw, bias, gain):
    ones1 = jnp.full((128, 128), 1.0 / 128, BF16)
    w_out = centred_columns(ew[0, 2]).astype(BF16)
    w_last = centred_columns(nw[0, 2]).astype(BF16)
    w_node = jnp.concatenate([nw[0, 0], nw[0, 1]], axis=0)
    mats = (ew[0, 0], block_diag(w_out), block_diag(ones1), w_node, w_last, ones1)
    b = bias[0]
    b_out = b[1:2] - jnp.mean(b[1:2])
    b_last = b[3:4] - jnp.mean(b[3:4])
    g = gain[0]
    rows = (b[0:1], jnp.concatenate([b_out, b_out], axis=1), g[0:1], b[2:3], b_last, g[1:2])
    return mats, rows


def pool(assign, rows_value, groups):
    lanes = lax.broadcasted_iota(jnp.int32, (groups, assign.shape[1]), 0)
    member = (lanes == assign).astype(BF16)
    return dot(member, rows_value)


def outgoing_kernel(x_ref, send_ref, ew_ref, own_ref, *out_refs):
    sender = dot(x_ref[...], ew_ref[0, 1]).astype(BF16)
    own_ref[...] = sender
    ids = send_ref[0].T
    for k, out in enumerate(out_refs):
        out[...] = dot(one_hot(ids[:, k : k + 1], sender.shape[0]), sender).astype(BF16)


def fine_kernel(
    x_ref, nbr_ref, assign_ref, own_ref, h0, h1, h2, h3, ew, nw, bias, gain, ew1,
    mid_ref, coarse_ref, sender_ref, table, pooled, *, block
):
    rows_total = x_ref.shape[0]
    groups = coarse_ref.shape[0]
    fill_table(table, [own_ref, h0, h1, h2, h3])
    mats, rows = level_params(ew, nw, bias, gain)
    pooled[...] = jnp.zeros_like(pooled)
    blank = 2 * table.shape[0]

    def step(j, carry):
        here = pl.ds(pl.multiple_of(j * block, block), block)
        x = x_ref[here, :]
        nbr = nbr_ref[:, here]
        mid = level_block(x, nbr, table, blank, mats, rows).astype(BF16)
        mid_ref[here, :] = mid
        pooled[...] += pool(assign_ref[:, here], mid, groups)
        return carry

    lax.fori_loop(0, rows_total // block, step, 0)
    coarse = (pooled[...] * 0.25).astype(BF16)
    coarse_ref[...] = coarse
    sender_ref[...] = dot(coarse, ew1[0, 1]).astype(BF16)


def coarse_kernel(
    x_ref, nbr_ref, assign_ref, s0, s1, s2, s3, s4, ew, nw, bias, gain, ew1,
    mid_ref, coarse_ref, sender_ref, table, *, block
):
    groups = coarse_ref.shape[0]
    fill_table(table, [s0, s1, s2, s3, s4])
    mats, rows = level_params(ew, nw, bias, gain)
    blank = 2 * table.shape[0]
    mid = level_block(x_ref[...], nbr_ref[...], table, blank, mats, rows).astype(BF16)
    mid_ref[...] = mid
    coarse = (pool(assign_ref[...], mid, groups) * 0.25).astype(BF16)
    coarse_ref[...] = coarse
    sender_ref[...] = dot(coarse, ew1[0, 1]).astype(BF16)


def coarsest_kernel(
    x_ref, nbr_ref, s0, s1, s2, s3, s4, s5, s6, ew, nw, bias, gain,
    fine_ref, coarse_ref, fine_assign, coarse_assign, out_ref, table
):
    fill_table(table, [s0, s1, s2, s3, s4, s5, s6])
    mats, rows = level_params(ew, nw, bias, gain)
    blank = 2 * table.shape[0]
    top = level_block(x_ref[...], nbr_ref[...], table, blank, mats, rows).astype(BF16)
    coarse = coarse_ref[...].astype(F32) + spread(coarse_assign[...], top)
    coarse = coarse.astype(BF16)
    out_ref[...] = (fine_ref[...].astype(F32) + spread(fine_assign[...], coarse)).astype(BF16)


def spread(assign, values):
    lanes = lax.broadcasted_iota(jnp.int32, (values.shape[0], assign.shape[1]), 0)
    member = (lanes == assign).astype(BF16)
    return lax.dot_general(member, values, (((0,), (0,)), ((), ())), preferred_element_type=F32)


def whole(shape):
    return pl.BlockSpec(shape, lambda *_: (0,) * len(shape))


def level_of(level, shape):
    return pl.BlockSpec((1,) + tuple(shape[1:]), lambda *_: (level,) + (0,) * (len(shape) - 1))


def call(kernel, operands, levels, outs, scratch, flops, name):
    specs = [
        whole(o.shape) if level is None else level_of(level, o.shape)
        for o, level in zip(operands, levels)
    ]
    moved = sum(o.size * o.dtype.itemsize for o in operands)
    return pl.pallas_call(
        kernel,
        grid=(1,),
        in_specs=specs,
        out_specs=[whole(s) for s in outs],
        out_shape=[jax.ShapeDtypeStruct(s, BF16) for s in outs],
        scratch_shapes=scratch,
        compiler_params=pltpu.CompilerParams(vmem_limit_bytes=VMEM_BYTES),
        cost_estimate=pl.CostEstimate(flops=flops, bytes_accessed=moved, transcendentals=0),
        name=name,
    )(*operands)


def on_device(
    node_features,
    fine_neighbors,
    send_rows,
    coarse_neighbors,
    coarsest_neighbors,
    fine_assign,
    coarse_assign,
    edge_weights,
    node_weights,
    biases,
    gains,
):
    fine_rows, width = node_features.shape
    coarse_rows = coarse_neighbors.shape[0]
    top_rows = coarsest_neighbors.shape[0]
    halo = send_rows.shape[2]
    fine_assign = fine_assign.reshape(1, -1)
    coarse_assign = coarse_assign.reshape(1, -1)
    params = [edge_weights, node_weights, biases, gains]

    own, *outgoing = call(
        outgoing_kernel,
        [node_features, send_rows, edge_weights],
        [None, None, 0],
        [(fine_rows, width)] + [(halo, width)] * 4,
        [],
        2 * 4 * halo * fine_rows * width,
        "outgoing",
    )
    arrived = [
        ring_shift(outgoing[0], "wide", 1),
        ring_shift(outgoing[1], "wide", -1),
        ring_shift(outgoing[2], "narrow", 1),
        ring_shift(outgoing[3], "narrow", -1),
    ]
    table_half = (fine_rows + 4 * halo) // 2
    fine_mid, coarse_in, sender = call(
        functools.partial(fine_kernel, block=256),
        [node_features, fine_neighbors.T, fine_assign, own] + arrived + params + [edge_weights],
        [None] * 8 + [0, 0, 0, 0, 1],
        [(fine_rows, width), (coarse_rows, width), (coarse_rows, width)],
        [pltpu.VMEM((table_half, 2 * width), BF16), pltpu.VMEM((coarse_rows, width), F32)],
        2 * 8 * fine_rows * table_half * 2 * width,
        "fine_level",
    )
    arrived = [sender]
    for axis in ("wide", "narrow"):
        for bit in range(2):
            arrived.append(from_partner(sender, axis, bit))
    table_half = 5 * coarse_rows // 2
    coarse_mid, top_in, sender = call(
        functools.partial(coarse_kernel, block=coarse_rows),
        [coarse_in, coarse_neighbors.T, coarse_assign] + arrived + params + [edge_weights],
        [None] * 8 + [1, 1, 1, 1, 2],
        [(coarse_rows, width), (top_rows, width), (top_rows, width)],
        [pltpu.VMEM((table_half, 2 * width), BF16)],
        2 * 8 * coarse_rows * table_half * 2 * width,
        "coarse_level",
    )
    wide_bits = lax.axis_size("wide").bit_length() - 1
    arrived = [sender] + [from_partner(sender, "wide", bit) for bit in range(wide_bits)]
    table_half = (wide_bits + 1) * top_rows // 2
    (result,) = call(
        coarsest_kernel,
        [top_in, coarsest_neighbors.T]
        + arrived
        + params
        + [fine_mid, coarse_mid, fine_assign, coarse_assign],
        [None] * (3 + wide_bits) + [2, 2, 2, 2] + [None] * 4,
        [(fine_rows, width)],
        [pltpu.VMEM((table_half, 2 * width), BF16)],
        2 * fine_rows * coarse_rows * width,
        "coarsest_level",
    )
    return result


def solution(mesh):
    rows = P(("wide", "narrow"), None)
    flat = P(("wide", "narrow"))
    in_specs = (rows, rows, P(("wide", "narrow"), None, None), rows, rows, flat, flat) + (P(),) * 4
    return jax.shard_map(
        on_device, mesh=mesh, in_specs=in_specs, out_specs=rows, check_vma=False
    )
```

```python
import functools

import jax
import jax.numpy as jnp
from jax import lax
from jax.experimental import pallas as pl
from jax.experimental.pallas import tpu as pltpu
from jax.sharding import PartitionSpec as P

F32 = jnp.float32
BF16 = jnp.bfloat16
I16 = jnp.int16
VMEM_BYTES = 48 * 1024 * 1024


def exchange(block, axis, pairs):
    route = [(i, j) for i, j in pairs] + [(j, i) for i, j in pairs]
    return lax.ppermute(block, axis, route)


def from_partner(block, axis, apart):
    count = lax.axis_size(axis)
    return lax.ppermute(block, axis, [(i, i ^ (1 << apart)) for i in range(count)])


def dot(a, b):
    return jnp.dot(a, b, preferred_element_type=F32)


def one_hot(column, width):
    lanes = lax.broadcasted_iota(jnp.int32, (column.shape[0], width), 1)
    return (column == lanes).astype(BF16)


def centred_columns(matrix):
    wide = matrix.astype(F32)
    return wide - jnp.mean(wide, axis=-1, keepdims=True)


def block_diag(matrix):
    zero = jnp.zeros_like(matrix)
    return jnp.concatenate(
        [jnp.concatenate([matrix, zero], axis=1), jnp.concatenate([zero, matrix], axis=1)], axis=0
    )


def fill_table(table, pieces):
    half = table.shape[0]
    start = 0
    for piece in pieces:
        rows = piece.shape[0]
        cut = min(rows, max(0, half - start))
        if cut > 0:
            table[start : start + cut, 0:128] = piece[0:cut]
        if cut < rows:
            low = start + cut - half
            table[low : low + rows - cut, 128:256] = piece[cut:rows]
        start += rows
    if start < 2 * half:
        table[start - half : half, 128:256] = jnp.zeros((2 * half - start, 128), BF16)


def lane_broadcast(row):
    tiles = [
        jnp.broadcast_to(row[:, b : b + 128], (128, 128)).astype(I16).T
        for b in range(0, row.shape[1], 128)
    ]
    return jnp.concatenate(tiles, axis=0) if len(tiles) > 1 else tiles[0]


def one_hot_lanes(code, width):
    parts = []
    for start in range(0, width, 128):
        lanes = lax.broadcasted_iota(I16, code.shape, 1) + I16(start)
        parts.append(jnp.where(code == lanes, BF16(1), BF16(0)))
    return jnp.concatenate(parts, axis=1)


def edge_sums(x, nbr, table, blank, mats, rows):
    w_recv, w_out2, ones2 = mats[:3]
    b_hid, b_out2, gain_e = rows[:3]
    half = table.shape[0]
    block = x.shape[0]
    slots = nbr.shape[0]
    receive = dot(x, w_recv) + b_hid
    code = jnp.concatenate([lane_broadcast(nbr[k : k + 1]) for k in range(slots)], axis=0)
    low = jnp.where(code >= I16(half), code - I16(half), code)
    got = dot(one_hot_lanes(low, half), table[...]).astype(BF16)
    sent = jnp.where(code >= I16(half), got[:, 128:256], got[:, 0:128]).astype(F32)
    hid = jnp.maximum(jnp.concatenate([receive] * slots, axis=0) + sent, 0.0).astype(BF16)
    hid = jnp.where(code < I16(blank), hid, BF16(0))
    split = slots // 2 * block
    c = dot(jnp.concatenate([hid[:split], hid[split:]], axis=1), w_out2) + b_out2
    var = dot((c * c).astype(BF16), ones2)
    m = c * lax.rsqrt(var + 1e-5)
    m = m[:, 0:128] + m[:, 128:256]
    total = m[0:block]
    for k in range(1, slots // 2):
        total = total + m[k * block : (k + 1) * block]
    bias_row = b_out2[:, 0:128]
    square = jnp.broadcast_to((bias_row * bias_row).astype(BF16), (16, 128))
    empty = bias_row * lax.rsqrt(dot(square, ones2[0:128, 0:128])[0:1] + 1e-5)
    missing = jnp.sum((nbr >= blank).astype(F32), axis=0, keepdims=True)
    missing = jnp.broadcast_to(missing, (8, block)).T[:, 0:1]
    return ((total - missing * empty) * gain_e).astype(BF16)


def node_step(x, summed, mats, rows):
    w_node, w_last, ones1 = mats[3:]
    b_node, b_last, gain_n = rows[3:]
    upd = jnp.maximum(dot(jnp.concatenate([x, summed], axis=1), w_node) + b_node, 0.0).astype(BF16)
    c = dot(upd, w_last) + b_last
    var = dot((c * c).astype(BF16), ones1)
    return (x.astype(F32) + c * lax.rsqrt(var + 1e-5) * gain_n).astype(BF16)


def level_params(ew, nw, bias, gain):
    ones1 = jnp.full((128, 128), 1.0 / 128, BF16)
    w_out = centred_columns(ew[0, 2]).astype(BF16)
    w_last = centred_columns(nw[0, 2]).astype(BF16)
    w_node = jnp.concatenate([nw[0, 0], nw[0, 1]], axis=0)
    mats = (ew[0, 0], block_diag(w_out), block_diag(ones1), w_node, w_last, ones1)
    b = bias[0]
    b_out = b[1:2] - jnp.mean(b[1:2])
    b_last = b[3:4] - jnp.mean(b[3:4])
    g = gain[0]
    rows = (b[0:1], jnp.concatenate([b_out, b_out], axis=1), g[0:1], b[2:3], b_last, g[1:2])
    return mats, rows


def pool(assign, rows_value, groups):
    lanes = lax.broadcasted_iota(jnp.int32, (groups, assign.shape[1]), 0)
    member = (lanes == assign).astype(BF16)
    return dot(member, rows_value)


def outgoing_kernel(par_ref, x_ref, send_ref, *out_refs):
    lists = send_ref[0].T
    x = x_ref[...]
    for axis in range(2):
        odd = par_ref[axis] == 1
        up, down = lists[:, 2 * axis : 2 * axis + 1], lists[:, 2 * axis + 1 : 2 * axis + 2]
        for k, ids in enumerate((jnp.where(odd, down, up), jnp.where(odd, up, down))):
            out_refs[2 * axis + k][...] = dot(one_hot(ids, x.shape[0]), x).astype(BF16)


def fine_kernel(
    par_ref, x_ref, nbr_ref, assign_ref, h1, h2, h3, h0, ew, nw, bias, gain, ew1,
    mid_ref, coarse_ref, sender_ref, table, sums, *, block
):
    rows_total = x_ref.shape[0]
    groups = coarse_ref.shape[0]
    x = x_ref[...]
    pieces = [x]
    for axis, (first, second) in enumerate(((h0, h1), (h2, h3))):
        odd = par_ref[axis] == 1
        first, second = first[...], second[...]
        pieces += [jnp.where(odd, first, second), jnp.where(odd, second, first)]
    fill_table(table, [dot(piece, ew[0, 1]).astype(BF16) for piece in pieces])
    mats, rows = level_params(ew, nw, bias, gain)
    blank = sum(piece.shape[0] for piece in pieces)

    def step(j, carry):
        here = pl.ds(pl.multiple_of(j * block, block), block)
        sums[here, :] = edge_sums(x_ref[here, :], nbr_ref[:, here], table, blank, mats, rows)
        return carry

    lax.fori_loop(0, rows_total // block, step, 0)
    mid = node_step(x, sums[...], mats, rows)
    mid_ref[...] = mid
    coarse = (pool(assign_ref[...], mid, groups) * 0.25).astype(BF16)
    coarse_ref[...] = coarse
    sender_ref[...] = dot(coarse, ew1[0, 1]).astype(BF16)


def coarse_kernel(
    x_ref, nbr_ref, assign_ref, s0, s4, s3, s2, s1, ew, nw, bias, gain, ew1,
    mid_ref, coarse_ref, sender_ref, table
):
    groups = coarse_ref.shape[0]
    fill_table(table, [s0, s1, s2, s3, s4])
    mats, rows = level_params(ew, nw, bias, gain)
    x = x_ref[...]
    sums = edge_sums(x, nbr_ref[...], table, 5 * x.shape[0], mats, rows)
    mid = node_step(x, sums, mats, rows)
    mid_ref[...] = mid
    coarse = (pool(assign_ref[...], mid, groups) * 0.25).astype(BF16)
    coarse_ref[...] = coarse
    sender_ref[...] = dot(coarse, ew1[0, 1]).astype(BF16)


def coarsest_kernel(
    x_ref, nbr_ref, s0, s4, s6, s3, s5, s2, s1, ew, nw, bias, gain,
    fine_ref, coarse_ref, fine_assign, coarse_assign, out_ref, table
):
    pieces = [s0, s1, s2, s3, s4, s5, s6]
    fill_table(table, pieces)
    mats, rows = level_params(ew, nw, bias, gain)
    count = x_ref.shape[0]
    blank = len(pieces) * count
    extra = -count % 128
    x = jnp.concatenate([x_ref[...], jnp.zeros((extra, 128), BF16)], axis=0)
    nbr = jnp.concatenate([nbr_ref[...], jnp.full((8, extra), blank, jnp.int32)], axis=1)
    top = node_step(x, edge_sums(x, nbr, table, blank, mats, rows), mats, rows)
    coarse = coarse_ref[...].astype(F32) + spread(coarse_assign[...], top)
    coarse = coarse.astype(BF16)
    out_ref[...] = (fine_ref[...].astype(F32) + spread(fine_assign[...], coarse)).astype(BF16)


def spread(assign, values):
    return dot(one_hot_lanes(lane_broadcast(assign), values.shape[0]), values)


def whole(shape):
    return pl.BlockSpec(shape, lambda *_: (0,) * len(shape))


def level_of(level, shape):
    return pl.BlockSpec((1,) + tuple(shape[1:]), lambda *_: (level,) + (0,) * (len(shape) - 1))


def call(kernel, operands, specs, outs, scratch, flops, name):
    moved = sum(o.size * o.dtype.itemsize for o in operands)
    specs = [
        whole(o.shape) if spec is None else level_of(spec, o.shape) if isinstance(spec, int) else spec
        for o, spec in zip(operands, specs)
    ]
    return pl.pallas_call(
        kernel,
        grid=(1,),
        in_specs=specs,
        out_specs=[whole(s) for s in outs],
        out_shape=[jax.ShapeDtypeStruct(s, BF16) for s in outs],
        scratch_shapes=scratch,
        compiler_params=pltpu.CompilerParams(vmem_limit_bytes=VMEM_BYTES),
        cost_estimate=pl.CostEstimate(flops=flops, bytes_accessed=moved, transcendentals=0),
        name=name,
    )(*operands)


def on_device(
    node_features,
    fine_neighbors,
    send_rows,
    coarse_neighbors,
    coarsest_neighbors,
    fine_assign,
    coarse_assign,
    edge_weights,
    node_weights,
    biases,
    gains,
):
    fine_rows, width = node_features.shape
    coarse_rows = coarse_neighbors.shape[0]
    top_rows = coarsest_neighbors.shape[0]
    halo = send_rows.shape[2]
    fine_assign = fine_assign.reshape(1, -1)
    coarse_assign = coarse_assign.reshape(1, -1)
    params = [edge_weights, node_weights, biases, gains]
    wide, narrow = lax.axis_size("wide"), lax.axis_size("narrow")
    wide_bits = wide.bit_length() - 1
    parity = jnp.stack([lax.axis_index("wide") % 2, lax.axis_index("narrow") % 2])
    smem = pl.BlockSpec(memory_space=pltpu.SMEM)

    outgoing = call(
        outgoing_kernel,
        [parity, node_features, send_rows],
        [smem, None, None],
        [(halo, width)] * 4,
        [],
        2 * 4 * halo * fine_rows * width,
        "outgoing",
    )
    odd_pairs = [(i, i + 1) for i in range(1, wide - 1, 2)]
    even_pairs = [(i, i + 1) for i in range(0, wide, 2)]
    odd_narrow = [(i, i + 1) for i in range(1, narrow - 1, 2)]
    even_narrow = [(i, i + 1) for i in range(0, narrow, 2)]
    from_odd = exchange(outgoing[1], "wide", odd_pairs)
    from_even_n = exchange(outgoing[2], "narrow", even_narrow)
    from_odd_n = exchange(outgoing[3], "narrow", odd_narrow)
    from_even = exchange(outgoing[0], "wide", even_pairs)
    table_half = (fine_rows + 4 * halo) // 2
    fine_mid, coarse_in, sender = call(
        functools.partial(fine_kernel, block=512),
        [parity, node_features, fine_neighbors.T, fine_assign]
        + [from_odd, from_even_n, from_odd_n, from_even]
        + params
        + [edge_weights],
        [smem] + [None] * 7 + [0, 0, 0, 0, 1],
        [(fine_rows, width), (coarse_rows, width), (coarse_rows, width)],
        [pltpu.VMEM((table_half, 2 * width), BF16), pltpu.VMEM((fine_rows, width), BF16)],
        2 * 8 * fine_rows * table_half * 2 * width,
        "fine_level",
    )
    far_n = from_partner(sender, "narrow", 1)
    near_n = from_partner(sender, "narrow", 0)
    far_w = from_partner(sender, "wide", 1)
    near_w = from_partner(sender, "wide", 0)
    table_half = -(-5 * coarse_rows // 256) * 128
    coarse_mid, top_in, sender = call(
        coarse_kernel,
        [coarse_in, coarse_neighbors.T, coarse_assign, sender, far_n, near_n, far_w, near_w]
        + params
        + [edge_weights],
        [None] * 8 + [1, 1, 1, 1, 2],
        [(coarse_rows, width), (top_rows, width), (top_rows, width)],
        [pltpu.VMEM((table_half, 2 * width), BF16)],
        2 * 8 * coarse_rows * table_half * 2 * width,
        "coarse_level",
    )
    arrived = [from_partner(sender, "wide", bit) for bit in (3, 5, 2, 4, 1, 0)]
    table_half = -(-(wide_bits + 1) * top_rows // 256) * 128
    (result,) = call(
        coarsest_kernel,
        [top_in, coarsest_neighbors.T, sender]
        + arrived
        + params
        + [fine_mid, coarse_mid, fine_assign, coarse_assign],
        [None] * (3 + wide_bits) + [2, 2, 2, 2] + [None] * 4,
        [(fine_rows, width)],
        [pltpu.VMEM((table_half, 2 * width), BF16)],
        2 * fine_rows * coarse_rows * width,
        "coarsest_level",
    )
    return result


def solution(mesh):
    rows = P(("wide", "narrow"), None)
    flat = P(("wide", "narrow"))
    in_specs = (rows, rows, P(("wide", "narrow"), None, None), rows, rows, flat, flat) + (P(),) * 4
    return jax.shard_map(
        on_device, mesh=mesh, in_specs=in_specs, out_specs=rows, check_vma=False
    )
```

```python
import functools

import jax
import jax.numpy as jnp
from jax import lax
from jax.experimental import pallas as pl
from jax.experimental.pallas import tpu as pltpu
from jax.sharding import PartitionSpec as P

F32 = jnp.float32
BF16 = jnp.bfloat16
I16 = jnp.int16
VMEM_BYTES = 24 * 1024 * 1024
LARGE = 62 * 1024 * 1024


def exchange(block, axis, pairs):
    route = [(i, j) for i, j in pairs] + [(j, i) for i, j in pairs]
    return lax.ppermute(block, axis, route)


def from_partner(block, axis, apart):
    count = lax.axis_size(axis)
    return lax.ppermute(block, axis, [(i, i ^ (1 << apart)) for i in range(count)])


def dot(a, b):
    return jnp.dot(a, b, preferred_element_type=F32)


def one_hot(column, width):
    lanes = lax.broadcasted_iota(jnp.int32, (column.shape[0], width), 1)
    return (column == lanes).astype(BF16)


def centred_columns(matrix):
    wide = matrix.astype(F32)
    return wide - jnp.mean(wide, axis=-1, keepdims=True)


def block_diag(matrix):
    zero = jnp.zeros_like(matrix)
    return jnp.concatenate(
        [jnp.concatenate([matrix, zero], axis=1), jnp.concatenate([zero, matrix], axis=1)], axis=0
    )


def fill_table(table, pieces):
    half = table.shape[0]
    start = 0
    for piece in pieces:
        rows = piece.shape[0]
        cut = min(rows, max(0, half - start))
        if cut > 0:
            table[start : start + cut, 0:128] = piece[0:cut]
        if cut < rows:
            low = start + cut - half
            table[low : low + rows - cut, 128:256] = piece[cut:rows]
        start += rows
    if start < half:
        table[start:half, 0:128] = jnp.zeros((half - start, 128), BF16)
    gap = max(start - half, 0)
    if gap < half:
        table[gap:half, 128:256] = jnp.zeros((half - gap, 128), BF16)


def lane_broadcast(row):
    tiles = [
        jnp.broadcast_to(row[:, b : b + 128], (128, 128)).astype(I16).T
        for b in range(0, row.shape[1], 128)
    ]
    return jnp.concatenate(tiles, axis=0) if len(tiles) > 1 else tiles[0]


def one_hot_lanes(code, width):
    parts = []
    for start in range(0, width, 128):
        lanes = lax.broadcasted_iota(I16, code.shape, 1) + I16(start)
        parts.append(jnp.where(code == lanes, BF16(1), BF16(0)))
    return jnp.concatenate(parts, axis=1)


def spread_slots(nbr):
    return jnp.concatenate([lane_broadcast(nbr[k : k + 1]) for k in range(nbr.shape[0])], axis=0)


def picked_rows(code, table):
    half = table.shape[0]
    high = code >= I16(half)
    low = jnp.where(high, code - I16(half), code)
    got = dot(one_hot_lanes(low, half), table[...]).astype(BF16)
    return jnp.where(high, got[:, 128:256], got[:, 0:128])


def edge_sums(x, nbr, table, first, partial, blank, mats, rows):
    w_recv, w_out2, ones2 = mats[:3]
    b_hid, b_out2, gain_e = rows[:3]
    block = x.shape[0]
    slots = nbr.shape[0]
    receive = dot(x, w_recv) + b_hid
    code = spread_slots(nbr)
    sent = picked_rows(code - I16(first) if first else code, table)
    if partial is not None:
        sent = sent + partial
    sent = sent.astype(F32)
    hid = jnp.maximum(jnp.concatenate([receive] * slots, axis=0) + sent, 0.0).astype(BF16)
    hid = jnp.where(code < I16(blank), hid, BF16(0))
    split = slots // 2 * block
    c = dot(jnp.concatenate([hid[:split], hid[split:]], axis=1), w_out2) + b_out2
    var = dot((c * c).astype(BF16), ones2)
    m = c * lax.rsqrt(var + 1e-5)
    m = m[:, 0:128] + m[:, 128:256]
    total = m[0:block]
    for k in range(1, slots // 2):
        total = total + m[k * block : (k + 1) * block]
    bias_row = b_out2[:, 0:128]
    square = jnp.broadcast_to((bias_row * bias_row).astype(BF16), (16, 128))
    empty = bias_row * lax.rsqrt(dot(square, ones2[0:128, 0:128])[0:1] + 1e-5)
    missing = jnp.sum((nbr >= blank).astype(F32), axis=0, keepdims=True)
    missing = jnp.broadcast_to(missing, (8, block)).T[:, 0:1]
    return ((total - missing * empty) * gain_e).astype(BF16)


def node_step(x, summed, mats, rows):
    w_node, w_last, ones1 = mats[3:]
    b_node, b_last, gain_n = rows[3:]
    upd = jnp.maximum(dot(jnp.concatenate([x, summed], axis=1), w_node) + b_node, 0.0).astype(BF16)
    c = dot(upd, w_last) + b_last
    var = dot((c * c).astype(BF16), ones1)
    return (x.astype(F32) + c * lax.rsqrt(var + 1e-5) * gain_n).astype(BF16)


def level_weights(ew, nw, edge_ref, last_ref):
    edge_ref[...] = block_diag(centred_columns(ew[0, 2]).astype(BF16))
    last_ref[...] = centred_columns(nw[0, 2]).astype(BF16)


def level_params(ew, nw, bias, gain, w_out2, w_last):
    ones1 = jnp.full((128, 128), 1.0 / 128, BF16)
    w_node = jnp.concatenate([nw[0, 0], nw[0, 1]], axis=0)
    mats = (ew[0, 0], w_out2[...], block_diag(ones1), w_node, w_last[...], ones1)
    b = bias[0]
    b_out = b[1:2] - jnp.mean(b[1:2])
    b_last = b[3:4] - jnp.mean(b[3:4])
    g = gain[0]
    rows = (b[0:1], jnp.concatenate([b_out, b_out], axis=1), g[0:1], b[2:3], b_last, g[1:2])
    return mats, rows


def pool(assign, rows_value, groups):
    lanes = lax.broadcasted_iota(jnp.int32, (groups, assign.shape[1]), 0)
    member = (lanes == assign).astype(BF16)
    return dot(member, rows_value)


def outgoing_kernel(par_ref, x_hbm, send_hbm, *refs):
    out_refs, (x_ref, send_ref, sems) = refs[:4], refs[4:]
    copies = [
        pltpu.make_async_copy(send_hbm, send_ref, sems.at[0]),
        pltpu.make_async_copy(x_hbm, x_ref, sems.at[1]),
    ]
    for copy in copies:
        copy.start()
    for copy in copies:
        copy.wait()
    lists = []
    for axis in range(2):
        odd = par_ref[axis] == 1
        up, down = send_ref[0, 2 * axis : 2 * axis + 1], send_ref[0, 2 * axis + 1 : 2 * axis + 2]
        lists += [jnp.where(odd, down, up), jnp.where(odd, up, down)]
    code = lane_broadcast(jnp.concatenate(lists, axis=1))
    x = x_ref[...]
    half = x.shape[0] // 2
    high = code >= I16(half)
    low = jnp.where(high, code - I16(half), code)
    pair = jnp.concatenate([x[:half], x[half:]], axis=1)
    got = dot(one_hot_lanes(low, half), pair).astype(BF16)
    got = jnp.where(high, got[:, 128:256], got[:, 0:128])
    rows = out_refs[0].shape[0]
    for k, out in enumerate(out_refs):
        out[...] = got[k * rows : (k + 1) * rows]


def fine_ahead_kernel(
    x_ref, nbr_ref, ew, nw, own_ref, edge_ref, last_ref, part_ref, table
):
    own = dot(x_ref[...], ew[0, 1]).astype(BF16)
    own_ref[...] = own
    level_weights(ew, nw, edge_ref, last_ref)
    fill_table(table, [own])
    part_ref[...] = picked_rows(spread_slots(nbr_ref[:, : part_ref.shape[0] // 8]), table)


def fine_kernel(
    par_ref, x_ref, nbr_ref, assign_ref, h1, h2, h3, h0, own_ref, edge_ref, last_ref, part_ref,
    ew, nw, bias, gain, ew1,
    mid_ref, coarse_ref, sender_ref, table, near_table, sums, *, block
):
    x = x_ref[...]
    halo = []
    for axis, (first, second) in enumerate(((h0, h1), (h2, h3))):
        odd = par_ref[axis] == 1
        first, second = first[...], second[...]
        halo += [jnp.where(odd, first, second), jnp.where(odd, second, first)]
    halo = [dot(piece, ew[0, 1]).astype(BF16) for piece in halo]
    own = own_ref[...]
    fill_table(table, [own] + halo)
    fill_table(near_table, halo)
    mats, rows = level_params(ew, nw, bias, gain, edge_ref, last_ref)
    rows_total = x_ref.shape[0]
    blank = rows_total + sum(piece.shape[0] for piece in halo)
    done = part_ref.shape[0] // 8
    sums[0:done] = edge_sums(
        x[0:done], nbr_ref[:, 0:done], near_table, rows_total, part_ref[...], blank, mats, rows
    )

    def step(j, carry):
        here = pl.ds(pl.multiple_of(j * block, block), block)
        nbr = nbr_ref[:, here]
        sums[here, :] = edge_sums(x_ref[here, :], nbr, table, 0, None, blank, mats, rows)
        return carry

    lax.fori_loop(done // block, rows_total // block, step, 0)
    mid = node_step(x, sums[...], mats, rows)
    mid_ref[...] = mid
    coarse = (pool(assign_ref[...], mid, coarse_ref.shape[0]) * 0.25).astype(BF16)
    coarse_ref[...] = coarse
    sender_ref[...] = dot(coarse, ew1[0, 1]).astype(BF16)


def coarse_ahead_kernel(sender_ref, nbr_ref, ew, nw, edge_ref, last_ref, part_ref, table):
    level_weights(ew, nw, edge_ref, last_ref)
    fill_table(table, [sender_ref])
    part_ref[...] = picked_rows(spread_slots(nbr_ref[...]), table)


def coarse_kernel(
    x_ref, nbr_ref, assign_ref, s1, s2, s3, s4, edge_ref, last_ref, part_ref,
    ew, nw, bias, gain, ew1,
    mid_ref, coarse_ref, sender_ref, table
):
    fill_table(table, [s1, s2, s3, s4])
    mats, rows = level_params(ew, nw, bias, gain, edge_ref, last_ref)
    x = x_ref[...]
    count = x.shape[0]
    sums = edge_sums(x, nbr_ref[...], table, count, part_ref[...], 5 * count, mats, rows)
    mid = node_step(x, sums, mats, rows)
    mid_ref[...] = mid
    coarse = (pool(assign_ref[...], mid, coarse_ref.shape[0]) * 0.25).astype(BF16)
    coarse_ref[...] = coarse
    sender_ref[...] = dot(coarse, ew1[0, 1]).astype(BF16)


def padded_nbr(nbr_ref, blank):
    extra = -nbr_ref.shape[1] % 128
    return jnp.concatenate([nbr_ref[...], jnp.full((8, extra), blank, jnp.int32)], axis=1)


def coarsest_ahead_kernel(
    sender_ref, nbr_ref, fine_assign, coarse_assign, ew, nw,
    edge_ref, last_ref, part_ref, fine_ref, coarse_ref, table, *, blank
):
    level_weights(ew, nw, edge_ref, last_ref)
    fill_table(table, [sender_ref])
    part_ref[...] = picked_rows(spread_slots(padded_nbr(nbr_ref, blank)), table)
    fine_ref[...] = one_hot_lanes(lane_broadcast(fine_assign[...]), fine_ref.shape[1])
    coarse_ref[...] = one_hot_lanes(lane_broadcast(coarse_assign[...]), coarse_ref.shape[1])


def coarsest_kernel(
    x_ref, nbr_ref, s1, s2, s5, s3, s6, s4, edge_ref, last_ref, part_ref, fine_hot, coarse_hot,
    ew, nw, bias, gain, fine_ref, coarse_ref, out_ref, table
):
    pieces = [s1, s2, s3, s4, s5, s6]
    fill_table(table, pieces)
    mats, rows = level_params(ew, nw, bias, gain, edge_ref, last_ref)
    count = x_ref.shape[0]
    blank = (len(pieces) + 1) * count
    x = jnp.concatenate([x_ref[...], jnp.zeros((-count % 128, 128), BF16)], axis=0)
    nbr = padded_nbr(nbr_ref, blank)
    sums = edge_sums(x, nbr, table, count, part_ref[...], blank, mats, rows)
    top = node_step(x, sums, mats, rows)
    coarse = (coarse_ref[...].astype(F32) + dot(coarse_hot[...], top)).astype(BF16)
    out_ref[...] = (fine_ref[...].astype(F32) + dot(fine_hot[...], coarse)).astype(BF16)


def call(kernel, operands, specs, outs, scratch, flops, name, vmem_bytes=VMEM_BYTES):
    moved = sum(o.size * o.dtype.itemsize for o in operands)
    vmem = pl.BlockSpec(memory_space=pltpu.VMEM)

    def body(*refs):
        views = [
            ref.at[pl.ds(spec, 1)] if isinstance(spec, int) else ref for ref, spec in zip(refs, specs)
        ]
        kernel(*views, *refs[len(specs) :])

    return pl.pallas_call(
        body,
        in_specs=[vmem if spec is None or isinstance(spec, int) else spec for spec in specs],
        out_specs=[vmem] * len(outs),
        out_shape=[jax.ShapeDtypeStruct(s, BF16) for s in outs],
        scratch_shapes=scratch,
        compiler_params=pltpu.CompilerParams(vmem_limit_bytes=vmem_bytes),
        cost_estimate=pl.CostEstimate(flops=flops, bytes_accessed=moved, transcendentals=0),
        name=name,
    )(*operands)


def on_device(
    node_features,
    fine_neighbors,
    send_rows,
    coarse_neighbors,
    coarsest_neighbors,
    fine_assign,
    coarse_assign,
    edge_weights,
    node_weights,
    biases,
    gains,
):
    fine_rows, width = node_features.shape
    coarse_rows = coarse_neighbors.shape[0]
    top_rows = coarsest_neighbors.shape[0]
    halo = send_rows.shape[2]
    fine_assign = fine_assign.reshape(1, -1)
    coarse_assign = coarse_assign.reshape(1, -1)
    params = [edge_weights, node_weights, biases, gains]
    wide, narrow = lax.axis_size("wide"), lax.axis_size("narrow")
    parity = jnp.stack([lax.axis_index("wide") % 2, lax.axis_index("narrow") % 2])
    smem = pl.BlockSpec(memory_space=pltpu.SMEM)

    outgoing = call(
        outgoing_kernel,
        [parity, node_features, send_rows],
        [smem, pl.BlockSpec(memory_space=pltpu.HBM), pl.BlockSpec(memory_space=pltpu.HBM)],
        [(halo, width)] * 4,
        [
            pltpu.VMEM((fine_rows, width), BF16),
            pltpu.VMEM(send_rows.shape, jnp.int32),
            pltpu.SemaphoreType.DMA((2,)),
        ],
        2 * 4 * halo * fine_rows * width,
        "outgoing",
        LARGE,
    )
    block = 512
    ahead = 1 * block
    table = functools.partial(pltpu.VMEM, dtype=BF16)
    weights = [(2 * width, 2 * width), (width, width)]
    odd_pairs = [(i, i + 1) for i in range(1, wide - 1, 2)]
    even_pairs = [(i, i + 1) for i in range(0, wide, 2)]
    odd_narrow = [(i, i + 1) for i in range(1, narrow - 1, 2)]
    even_narrow = [(i, i + 1) for i in range(0, narrow, 2)]
    from_odd = exchange(outgoing[1], "wide", odd_pairs)
    from_even_n = exchange(outgoing[2], "narrow", even_narrow)
    from_odd_n = exchange(outgoing[3], "narrow", odd_narrow)
    from_even = exchange(outgoing[0], "wide", even_pairs)
    fine_ahead = call(
        fine_ahead_kernel,
        [node_features, fine_neighbors.T, edge_weights, node_weights],
        [None, None, 0, 0],
        [(fine_rows, width)] + weights + [(8 * ahead, width)],
        [table((fine_rows // 2, 2 * width))],
        2 * 8 * ahead * fine_rows * width,
        "fine_ahead",
    )
    fine_mid, coarse_in, sender = call(
        functools.partial(fine_kernel, block=block),
        [parity, node_features, fine_neighbors.T, fine_assign]
        + [from_odd, from_even_n, from_odd_n, from_even]
        + list(fine_ahead)
        + params
        + [edge_weights],
        [smem] + [None] * 11 + [0, 0, 0, 0, 1],
        [(fine_rows, width), (coarse_rows, width), (coarse_rows, width)],
        [
            table(((fine_rows + 4 * halo) // 2, 2 * width)),
            table((2 * halo, 2 * width)),
            table((fine_rows, width)),
        ],
        2 * 8 * fine_rows * (fine_rows + 4 * halo) * width,
        "fine_level",
    )
    far_n = from_partner(sender, "narrow", 1)
    near_n = from_partner(sender, "narrow", 0)
    far_w = from_partner(sender, "wide", 1)
    near_w = from_partner(sender, "wide", 0)
    coarse_ahead = call(
        coarse_ahead_kernel,
        [sender, coarse_neighbors.T, edge_weights, node_weights],
        [None, None, 1, 1],
        weights + [(8 * coarse_rows, width)],
        [table((-(-coarse_rows // 256) * 128, 2 * width))],
        2 * 8 * coarse_rows * coarse_rows * width,
        "coarse_ahead",
    )
    coarse_mid, top_in, sender = call(
        coarse_kernel,
        [coarse_in, coarse_neighbors.T, coarse_assign, near_w, far_w, near_n, far_n]
        + list(coarse_ahead)
        + params
        + [edge_weights],
        [None] * 10 + [1, 1, 1, 1, 2],
        [(coarse_rows, width), (top_rows, width), (top_rows, width)],
        [table((-(-4 * coarse_rows // 256) * 128, 2 * width))],
        2 * 8 * coarse_rows * 4 * coarse_rows * width,
        "coarse_level",
    )
    wide_bits = wide.bit_length() - 1
    arrived = [from_partner(sender, "wide", bit) for bit in (0, 1, 4, 2, 5, 3)]
    top_pad = -(-top_rows // 128) * 128
    coarsest_ahead = call(
        functools.partial(coarsest_ahead_kernel, blank=(wide_bits + 1) * top_rows),
        [sender, coarsest_neighbors.T, fine_assign, coarse_assign, edge_weights, node_weights],
        [None] * 4 + [2, 2],
        weights + [(8 * top_pad, width), (fine_rows, coarse_rows), (coarse_rows, top_pad)],
        [table((128, 2 * width))],
        2 * fine_rows * coarse_rows * width,
        "coarsest_ahead",
    )
    (result,) = call(
        coarsest_kernel,
        [top_in, coarsest_neighbors.T]
        + arrived
        + list(coarsest_ahead)
        + params
        + [fine_mid, coarse_mid],
        [None] * 13 + [2, 2, 2, 2] + [None] * 2,
        [(fine_rows, width)],
        [table((-(-wide_bits * top_rows // 256) * 128, 2 * width))],
        2 * fine_rows * coarse_rows * width,
        "coarsest_level",
    )
    return result


def solution(mesh):
    rows = P(("wide", "narrow"), None)
    flat = P(("wide", "narrow"))
    in_specs = (rows, rows, P(("wide", "narrow"), None, None), rows, rows, flat, flat) + (P(),) * 4
    return jax.shard_map(
        on_device, mesh=mesh, in_specs=in_specs, out_specs=rows, check_vma=False
    )
```

```python
import functools

import jax
import jax.numpy as jnp
from jax import lax
from jax.experimental import pallas as pl
from jax.experimental.pallas import tpu as pltpu
from jax.sharding import PartitionSpec as P

F32 = jnp.float32
BF16 = jnp.bfloat16
I16 = jnp.int16
VMEM_BYTES = 24 * 1024 * 1024


def exchange(block, axis, pairs):
    route = [(i, j) for i, j in pairs] + [(j, i) for i, j in pairs]
    return lax.ppermute(block, axis, route)


def from_partner(block, axis, apart):
    count = lax.axis_size(axis)
    return lax.ppermute(block, axis, [(i, i ^ (1 << apart)) for i in range(count)])


def dot(a, b):
    return jnp.dot(a, b, preferred_element_type=F32)


def one_hot(column, width):
    lanes = lax.broadcasted_iota(jnp.int32, (column.shape[0], width), 1)
    return (column == lanes).astype(BF16)


def centred_columns(matrix):
    wide = matrix.astype(F32)
    return wide - jnp.mean(wide, axis=-1, keepdims=True)


def block_diag(matrix):
    zero = jnp.zeros_like(matrix)
    return jnp.concatenate(
        [jnp.concatenate([matrix, zero], axis=1), jnp.concatenate([zero, matrix], axis=1)], axis=0
    )


def fill_table(table, pieces):
    half = table.shape[0]
    start = 0
    for piece in pieces:
        rows = piece.shape[0]
        cut = min(rows, max(0, half - start))
        if cut > 0:
            table[start : start + cut, 0:128] = piece[0:cut]
        if cut < rows:
            low = start + cut - half
            table[low : low + rows - cut, 128:256] = piece[cut:rows]
        start += rows
    if start < half:
        table[start:half, 0:128] = jnp.zeros((half - start, 128), BF16)
    gap = max(start - half, 0)
    if gap < half:
        table[gap:half, 128:256] = jnp.zeros((half - gap, 128), BF16)


def lane_broadcast(row):
    tiles = [
        jnp.broadcast_to(row[:, b : b + 128], (128, 128)).astype(I16).T
        for b in range(0, row.shape[1], 128)
    ]
    return jnp.concatenate(tiles, axis=0) if len(tiles) > 1 else tiles[0]


def one_hot_lanes(code, width):
    parts = []
    for start in range(0, width, 128):
        lanes = lax.broadcasted_iota(I16, code.shape, 1) + I16(start)
        parts.append(jnp.where(code == lanes, BF16(1), BF16(0)))
    return jnp.concatenate(parts, axis=1)


def spread_slots(nbr):
    return jnp.concatenate([lane_broadcast(nbr[k : k + 1]) for k in range(nbr.shape[0])], axis=0)


def picked_rows(code, table):
    half = table.shape[0]
    high = code >= I16(half)
    low = jnp.where(high, code - I16(half), code)
    got = dot(one_hot_lanes(low, half), table[...]).astype(BF16)
    return jnp.where(high, got[:, 128:256], got[:, 0:128])


def edge_sums(x, nbr, table, first, partial, blank, mats, rows):
    w_recv, w_out2, ones2 = mats[:3]
    b_hid, b_out2, gain_e, empty = rows[:4]
    block = x.shape[0]
    slots = nbr.shape[0]
    receive = dot(x, w_recv) + b_hid
    code = spread_slots(nbr)
    sent = picked_rows(code - I16(first) if first else code, table)
    if partial is not None:
        sent = sent + partial
    sent = sent.astype(F32)
    hid = jnp.maximum(jnp.concatenate([receive] * slots, axis=0) + sent, 0.0).astype(BF16)
    hid = jnp.where(code < I16(blank), hid, BF16(0))
    split = slots // 2 * block
    c = dot(jnp.concatenate([hid[:split], hid[split:]], axis=1), w_out2) + b_out2
    var = dot((c * c).astype(BF16), ones2)
    m = c * lax.rsqrt(var + 1e-5)
    m = m[:, 0:128] + m[:, 128:256]
    total = m[0:block]
    for k in range(1, slots // 2):
        total = total + m[k * block : (k + 1) * block]
    missing = jnp.sum((nbr >= blank).astype(F32), axis=0, keepdims=True)
    missing = jnp.broadcast_to(missing, (8, block)).T[:, 0:1]
    return ((total - missing * empty) * gain_e).astype(BF16)


def node_step(x, summed, mats, rows):
    w_node, w_last, ones1 = mats[3:]
    b_node, b_last, gain_n = rows[4:]
    upd = jnp.maximum(dot(jnp.concatenate([x, summed], axis=1), w_node) + b_node, 0.0).astype(BF16)
    c = dot(upd, w_last) + b_last
    var = dot((c * c).astype(BF16), ones1)
    return (x.astype(F32) + c * lax.rsqrt(var + 1e-5) * gain_n).astype(BF16)


def edge_weight(ew):
    return block_diag(centred_columns(ew[0, 2]).astype(BF16))


def last_weight(nw):
    return centred_columns(nw[0, 2]).astype(BF16)


def level_params(ew, nw, bias, gain, w_out2, w_last):
    ones1 = jnp.full((128, 128), 1.0 / 128, BF16)
    w_node = jnp.concatenate([nw[0, 0], nw[0, 1]], axis=0)
    mats = (ew[0, 0], w_out2[...], block_diag(ones1), w_node, w_last, ones1)
    b = bias[0]
    b_out = b[1:2] - jnp.mean(b[1:2])
    b_last = b[3:4] - jnp.mean(b[3:4])
    g = gain[0]
    square = jnp.broadcast_to((b_out * b_out).astype(BF16), (16, 128))
    empty = b_out * lax.rsqrt(dot(square, ones1)[0:1] + 1e-5)
    b_pair = jnp.concatenate([b_out, b_out], axis=1)
    rows = (b[0:1], b_pair, g[0:1], empty, b[2:3], b_last, g[1:2])
    return mats, rows


def pool(assign, rows_value, groups):
    lanes = lax.broadcasted_iota(jnp.int32, (groups, assign.shape[1]), 0)
    member = (lanes == assign).astype(BF16)
    return dot(member, rows_value)


def outgoing_kernel(par_ref, x_ref, send_ref, *out_refs):
    lists = []
    for axis in range(2):
        odd = par_ref[axis] == 1
        up, down = send_ref[0, 2 * axis : 2 * axis + 1], send_ref[0, 2 * axis + 1 : 2 * axis + 2]
        lists += [jnp.where(odd, down, up), jnp.where(odd, up, down)]
    code = lane_broadcast(jnp.concatenate(lists, axis=1))
    x = x_ref[...]
    out_refs[4][...] = x
    half = x.shape[0] // 2
    high = code >= I16(half)
    low = jnp.where(high, code - I16(half), code)
    pair = jnp.concatenate([x[:half], x[half:]], axis=1)
    got = dot(one_hot_lanes(low, half), pair).astype(BF16)
    got = jnp.where(high, got[:, 128:256], got[:, 0:128])
    rows = out_refs[0].shape[0]
    for k, out in enumerate(out_refs[:4]):
        out[...] = got[k * rows : (k + 1) * rows]


def fine_ahead_kernel(
    x_ref, nbr_ref, ew, own_ref, edge_ref, part_ref, table
):
    own = dot(x_ref[...], ew[0, 1]).astype(BF16)
    own_ref[...] = own
    edge_ref[...] = edge_weight(ew)
    fill_table(table, [own])
    part_ref[...] = picked_rows(spread_slots(nbr_ref[:, : part_ref.shape[0] // 8]), table)


def fine_kernel(
    par_ref, x_ref, nbr_ref, assign_ref, h1, h2, h3, h0, own_ref, edge_ref, part_ref,
    ew, nw, bias, gain, ew1,
    mid_ref, coarse_ref, sender_ref, table, near_table, sums, *, block
):
    x = x_ref[...]
    halo = []
    for axis, (first, second) in enumerate(((h0, h1), (h2, h3))):
        odd = par_ref[axis] == 1
        first, second = first[...], second[...]
        halo += [jnp.where(odd, first, second), jnp.where(odd, second, first)]
    halo = [dot(jnp.concatenate(halo, axis=0), ew[0, 1]).astype(BF16)]
    own = own_ref[...]
    fill_table(table, [own] + halo)
    fill_table(near_table, halo)
    mats, rows = level_params(ew, nw, bias, gain, edge_ref, last_weight(nw))
    rows_total = x_ref.shape[0]
    blank = rows_total + sum(piece.shape[0] for piece in halo)
    done = part_ref.shape[0] // 8
    sums[0:done] = edge_sums(
        x[0:done], nbr_ref[:, 0:done], near_table, rows_total, part_ref[...], blank, mats, rows
    )

    def step(j, carry):
        here = pl.ds(pl.multiple_of(j * block, block), block)
        nbr = nbr_ref[:, here]
        sums[here, :] = edge_sums(x_ref[here, :], nbr, table, 0, None, blank, mats, rows)
        return carry

    lax.fori_loop(done // block, rows_total // block, step, 0)
    mid = node_step(x, sums[...], mats, rows)
    mid_ref[...] = mid
    coarse = (pool(assign_ref[...], mid, coarse_ref.shape[0]) * 0.25).astype(BF16)
    coarse_ref[...] = coarse
    sender_ref[...] = dot(coarse, ew1[0, 1]).astype(BF16)


def coarse_ahead_kernel(sender_ref, nbr_ref, ew, nw, edge_ref, last_ref, part_ref, table):
    edge_ref[...] = edge_weight(ew)
    last_ref[...] = last_weight(nw)
    fill_table(table, [sender_ref])
    part_ref[...] = picked_rows(spread_slots(nbr_ref[...]), table)


def coarse_kernel(
    x_ref, nbr_ref, assign_ref, s4, s3, s2, s1, edge_ref, last_ref, part_ref,
    ew, nw, bias, gain, ew1,
    mid_ref, coarse_ref, sender_ref, table
):
    fill_table(table, [s1, s2, s3, s4])
    mats, rows = level_params(ew, nw, bias, gain, edge_ref, last_ref[...])
    x = x_ref[...]
    count = x.shape[0]
    sums = edge_sums(x, nbr_ref[...], table, count, part_ref[...], 5 * count, mats, rows)
    mid = node_step(x, sums, mats, rows)
    mid_ref[...] = mid
    coarse = (pool(assign_ref[...], mid, coarse_ref.shape[0]) * 0.25).astype(BF16)
    coarse_ref[...] = coarse
    sender_ref[...] = dot(coarse, ew1[0, 1]).astype(BF16)


def padded_nbr(nbr_ref, blank):
    extra = -nbr_ref.shape[1] % 128
    return jnp.concatenate([nbr_ref[...], jnp.full((8, extra), blank, jnp.int32)], axis=1)


def coarsest_ahead_kernel(
    sender_ref, nbr_ref, fine_assign, coarse_assign, ew, nw,
    edge_ref, last_ref, part_ref, fine_ref, coarse_ref, table, *, blank
):
    edge_ref[...] = edge_weight(ew)
    last_ref[...] = last_weight(nw)
    fill_table(table, [sender_ref])
    part_ref[...] = picked_rows(spread_slots(padded_nbr(nbr_ref, blank)), table)
    fine_ref[...] = one_hot_lanes(lane_broadcast(fine_assign[...]), fine_ref.shape[1])
    coarse_ref[...] = one_hot_lanes(lane_broadcast(coarse_assign[...]), coarse_ref.shape[1])


def coarsest_kernel(
    x_ref, nbr_ref, s2, s1, s4, s6, s3, s5, edge_ref, last_ref, part_ref, fine_hot, coarse_hot,
    ew, nw, bias, gain, fine_ref, coarse_ref, out_ref, table
):
    pieces = [s1, s2, s3, s4, s5, s6]
    fill_table(table, pieces)
    mats, rows = level_params(ew, nw, bias, gain, edge_ref, last_ref[...])
    count = x_ref.shape[0]
    blank = (len(pieces) + 1) * count
    x = jnp.concatenate([x_ref[...], jnp.zeros((-count % 128, 128), BF16)], axis=0)
    nbr = padded_nbr(nbr_ref, blank)
    sums = edge_sums(x, nbr, table, count, part_ref[...], blank, mats, rows)
    top = node_step(x, sums, mats, rows)
    coarse = (coarse_ref[...].astype(F32) + dot(coarse_hot[...], top)).astype(BF16)
    out_ref[...] = (fine_ref[...].astype(F32) + dot(fine_hot[...], coarse)).astype(BF16)


def call(kernel, operands, specs, outs, scratch, flops, name, vmem_bytes=VMEM_BYTES):
    moved = sum(o.size * o.dtype.itemsize for o in operands)
    vmem = pl.BlockSpec(memory_space=pltpu.VMEM)

    def body(*refs):
        views = [
            ref.at[pl.ds(spec, 1)] if isinstance(spec, int) else ref for ref, spec in zip(refs, specs)
        ]
        kernel(*views, *refs[len(specs) :])

    return pl.pallas_call(
        body,
        in_specs=[vmem if spec is None or isinstance(spec, int) else spec for spec in specs],
        out_specs=[vmem] * len(outs),
        out_shape=[jax.ShapeDtypeStruct(s, BF16) for s in outs],
        scratch_shapes=scratch,
        compiler_params=pltpu.CompilerParams(vmem_limit_bytes=vmem_bytes),
        cost_estimate=pl.CostEstimate(flops=flops, bytes_accessed=moved, transcendentals=0),
        name=name,
    )(*operands)


def on_device(
    node_features,
    fine_neighbors,
    send_rows,
    coarse_neighbors,
    coarsest_neighbors,
    fine_assign,
    coarse_assign,
    edge_weights,
    node_weights,
    biases,
    gains,
):
    fine_rows, width = node_features.shape
    coarse_rows = coarse_neighbors.shape[0]
    top_rows = coarsest_neighbors.shape[0]
    halo = send_rows.shape[2]
    fine_assign = fine_assign.reshape(1, -1)
    coarse_assign = coarse_assign.reshape(1, -1)
    params = [edge_weights, node_weights, biases, gains]
    wide, narrow = lax.axis_size("wide"), lax.axis_size("narrow")
    parity = jnp.stack([lax.axis_index("wide") % 2, lax.axis_index("narrow") % 2])
    smem = pl.BlockSpec(memory_space=pltpu.SMEM)

    *outgoing, rows_kept = call(
        outgoing_kernel,
        [parity, node_features, send_rows],
        [smem, None, None],
        [(halo, width)] * 4 + [(fine_rows, width)],
        [],
        2 * 4 * halo * fine_rows * width,
        "outgoing",
    )
    block = 512
    ahead = 1 * block
    table = functools.partial(pltpu.VMEM, dtype=BF16)
    weights = [(2 * width, 2 * width), (width, width)]
    odd_pairs = [(i, (i + 1) % wide) for i in range(1, wide, 2)]
    even_pairs = [(i, i + 1) for i in range(0, wide, 2)]
    odd_narrow = [(i, (i + 1) % narrow) for i in range(1, narrow, 2)]
    even_narrow = [(i, i + 1) for i in range(0, narrow, 2)]
    from_odd = exchange(outgoing[1], "wide", odd_pairs)
    from_even_n = exchange(outgoing[2], "narrow", even_narrow)
    from_odd_n = exchange(outgoing[3], "narrow", odd_narrow)
    from_even = exchange(outgoing[0], "wide", even_pairs)
    fine_ahead = call(
        fine_ahead_kernel,
        [rows_kept, fine_neighbors.T, edge_weights],
        [None, None, 0],
        [(fine_rows, width), weights[0], (8 * ahead, width)],
        [table((fine_rows // 2, 2 * width))],
        2 * 8 * ahead * fine_rows * width,
        "fine_ahead",
    )
    fine_mid, coarse_in, sender = call(
        functools.partial(fine_kernel, block=block),
        [parity, rows_kept, fine_neighbors.T, fine_assign]
        + [from_odd, from_even_n, from_odd_n, from_even]
        + list(fine_ahead)
        + params
        + [edge_weights],
        [smem] + [None] * 10 + [0, 0, 0, 0, 1],
        [(fine_rows, width), (coarse_rows, width), (coarse_rows, width)],
        [
            table(((fine_rows + 4 * halo) // 2, 2 * width)),
            table((2 * halo, 2 * width)),
            table((fine_rows, width)),
        ],
        2 * 8 * fine_rows * (fine_rows + 4 * halo) * width,
        "fine_level",
    )
    far_n = from_partner(sender, "narrow", 1)
    near_n = from_partner(sender, "narrow", 0)
    far_w = from_partner(sender, "wide", 1)
    near_w = from_partner(sender, "wide", 0)
    coarse_ahead = call(
        coarse_ahead_kernel,
        [sender, coarse_neighbors.T, edge_weights, node_weights],
        [None, None, 1, 1],
        weights + [(8 * coarse_rows, width)],
        [table((-(-coarse_rows // 256) * 128, 2 * width))],
        2 * 8 * coarse_rows * coarse_rows * width,
        "coarse_ahead",
    )
    coarse_mid, top_in, sender = call(
        coarse_kernel,
        [coarse_in, coarse_neighbors.T, coarse_assign, far_n, near_n, far_w, near_w]
        + list(coarse_ahead)
        + params
        + [edge_weights],
        [None] * 10 + [1, 1, 1, 1, 2],
        [(coarse_rows, width), (top_rows, width), (top_rows, width)],
        [table((-(-4 * coarse_rows // 256) * 128, 2 * width))],
        2 * 8 * coarse_rows * 4 * coarse_rows * width,
        "coarse_level",
    )
    wide_bits = wide.bit_length() - 1
    arrived = [from_partner(sender, "wide", bit) for bit in (1, 0, 3, 5, 2, 4)]
    top_pad = -(-top_rows // 128) * 128
    coarsest_ahead = call(
        functools.partial(coarsest_ahead_kernel, blank=(wide_bits + 1) * top_rows),
        [sender, coarsest_neighbors.T, fine_assign, coarse_assign, edge_weights, node_weights],
        [None] * 4 + [2, 2],
        weights + [(8 * top_pad, width), (fine_rows, coarse_rows), (coarse_rows, top_pad)],
        [table((128, 2 * width))],
        2 * fine_rows * coarse_rows * width,
        "coarsest_ahead",
    )
    (result,) = call(
        coarsest_kernel,
        [top_in, coarsest_neighbors.T]
        + arrived
        + list(coarsest_ahead)
        + params
        + [fine_mid, coarse_mid],
        [None] * 13 + [2, 2, 2, 2] + [None] * 2,
        [(fine_rows, width)],
        [table((-(-wide_bits * top_rows // 256) * 128, 2 * width))],
        2 * fine_rows * coarse_rows * width,
        "coarsest_level",
    )
    return result


def solution(mesh):
    rows = P(("wide", "narrow"), None)
    flat = P(("wide", "narrow"))
    in_specs = (rows, rows, P(("wide", "narrow"), None, None), rows, rows, flat, flat) + (P(),) * 4
    return jax.shard_map(
        on_device, mesh=mesh, in_specs=in_specs, out_specs=rows, check_vma=False
    )
```

```python
import functools

import jax
import jax.numpy as jnp
from jax import lax
from jax.experimental import pallas as pl
from jax.experimental.pallas import tpu as pltpu
from jax.sharding import PartitionSpec as P

F32 = jnp.float32
BF16 = jnp.bfloat16
I16 = jnp.int16
VMEM_BYTES = 24 * 1024 * 1024


def exchange(block, axis, pairs):
    route = [(i, j) for i, j in pairs] + [(j, i) for i, j in pairs]
    return lax.ppermute(block, axis, route)


def from_partner(block, axis, apart):
    count = lax.axis_size(axis)
    return lax.ppermute(block, axis, [(i, i ^ (1 << apart)) for i in range(count)])


def dot(a, b):
    return jnp.dot(a, b, preferred_element_type=F32)


def one_hot(column, width):
    lanes = lax.broadcasted_iota(jnp.int32, (column.shape[0], width), 1)
    return (column == lanes).astype(BF16)


def centred_columns(matrix):
    wide = matrix.astype(F32)
    return wide - jnp.mean(wide, axis=-1, keepdims=True)


def block_diag(matrix):
    zero = jnp.zeros_like(matrix)
    return jnp.concatenate(
        [jnp.concatenate([matrix, zero], axis=1), jnp.concatenate([zero, matrix], axis=1)], axis=0
    )


def fill_table(table, pieces):
    half = table.shape[0]
    start = 0
    for piece in pieces:
        rows = piece.shape[0]
        cut = min(rows, max(0, half - start))
        if cut > 0:
            table[start : start + cut, 0:128] = piece[0:cut]
        if cut < rows:
            low = start + cut - half
            table[low : low + rows - cut, 128:256] = piece[cut:rows]
        start += rows
    if start < half:
        table[start:half, 0:128] = jnp.zeros((half - start, 128), BF16)
    gap = max(start - half, 0)
    if gap < half:
        table[gap:half, 128:256] = jnp.zeros((half - gap, 128), BF16)


def lane_broadcast(row):
    tiles = [
        jnp.broadcast_to(row[:, b : b + 128], (128, 128)).astype(I16).T
        for b in range(0, row.shape[1], 128)
    ]
    return jnp.concatenate(tiles, axis=0) if len(tiles) > 1 else tiles[0]


def one_hot_lanes(code, width):
    parts = []
    for start in range(0, width, 128):
        lanes = lax.broadcasted_iota(I16, code.shape, 1) + I16(start)
        parts.append(jnp.where(code == lanes, BF16(1), BF16(0)))
    return jnp.concatenate(parts, axis=1)


def spread_slots(nbr):
    return jnp.concatenate([lane_broadcast(nbr[k : k + 1]) for k in range(nbr.shape[0])], axis=0)


def picked_rows(code, table):
    half = table.shape[0]
    high = code >= I16(half)
    low = jnp.where(high, code - I16(half), code)
    got = dot(one_hot_lanes(low, half), table[...]).astype(BF16)
    return jnp.where(high, got[:, 128:256], got[:, 0:128])


def unit_rows(c):
    return c * lax.rsqrt(jnp.mean(c * c, axis=-1, keepdims=True) + 1e-5)


def edge_sums(x, nbr, table, first, partial, blank, mats, rows):
    w_recv, w_out2 = mats[:2]
    b_hid, b_out2, gain_e, empty = rows[:4]
    block = x.shape[0]
    slots = nbr.shape[0]
    receive = dot(x, w_recv) + b_hid
    code = spread_slots(nbr)
    sent = picked_rows(code - I16(first) if first else code, table)
    if partial is not None:
        sent = sent + partial
    sent = sent.astype(F32)
    hid = jnp.maximum(jnp.concatenate([receive] * slots, axis=0) + sent, 0.0).astype(BF16)
    hid = jnp.where(code < I16(blank), hid, BF16(0))
    split = slots // 2 * block
    c = dot(jnp.concatenate([hid[:split], hid[split:]], axis=1), w_out2) + b_out2
    m = unit_rows(c[:, 0:128]) + unit_rows(c[:, 128:256])
    total = m[0:block]
    for k in range(1, slots // 2):
        total = total + m[k * block : (k + 1) * block]
    missing = jnp.sum((nbr >= blank).astype(F32), axis=0, keepdims=True)
    missing = jnp.broadcast_to(missing, (8, block)).T[:, 0:1]
    return ((total - missing * empty) * gain_e).astype(BF16)


def node_step(x, summed, mats, rows):
    w_node, w_last = mats[2:]
    b_node, b_last, gain_n = rows[4:]
    upd = jnp.maximum(dot(jnp.concatenate([x, summed], axis=1), w_node) + b_node, 0.0).astype(BF16)
    return (x.astype(F32) + unit_rows(dot(upd, w_last) + b_last) * gain_n).astype(BF16)


def edge_weight(ew):
    return block_diag(centred_columns(ew[0, 2]).astype(BF16))


def last_weight(nw):
    return centred_columns(nw[0, 2]).astype(BF16)


def level_params(ew, nw, bias, gain, w_out2, w_last):
    w_node = jnp.concatenate([nw[0, 0], nw[0, 1]], axis=0)
    mats = (ew[0, 0], w_out2[...], w_node, w_last)
    b = bias[0]
    b_out = b[1:2] - jnp.mean(b[1:2])
    b_last = b[3:4] - jnp.mean(b[3:4])
    g = gain[0]
    b_pair = jnp.concatenate([b_out, b_out], axis=1)
    rows = (b[0:1], b_pair, g[0:1], unit_rows(b_out), b[2:3], b_last, g[1:2])
    return mats, rows


def pool(assign, rows_value, groups):
    lanes = lax.broadcasted_iota(jnp.int32, (groups, assign.shape[1]), 0)
    member = (lanes == assign).astype(BF16)
    return dot(member, rows_value)


def outgoing_kernel(par_ref, x_ref, send_ref, *out_refs):
    lists = []
    for axis in range(2):
        odd = par_ref[axis] == 1
        up, down = send_ref[0, 2 * axis : 2 * axis + 1], send_ref[0, 2 * axis + 1 : 2 * axis + 2]
        lists += [jnp.where(odd, down, up), jnp.where(odd, up, down)]
    code = lane_broadcast(jnp.concatenate(lists, axis=1))
    x = x_ref[...]
    out_refs[4][...] = x
    half = x.shape[0] // 2
    high = code >= I16(half)
    low = jnp.where(high, code - I16(half), code)
    pair = jnp.concatenate([x[:half], x[half:]], axis=1)
    got = dot(one_hot_lanes(low, half), pair).astype(BF16)
    got = jnp.where(high, got[:, 128:256], got[:, 0:128])
    rows = out_refs[0].shape[0]
    for k, out in enumerate(out_refs[:4]):
        out[...] = got[k * rows : (k + 1) * rows]


def fine_ahead_kernel(
    x_ref, nbr_ref, ew, own_ref, edge_ref, part_ref, table
):
    own = dot(x_ref[...], ew[0, 1]).astype(BF16)
    own_ref[...] = own
    edge_ref[...] = edge_weight(ew)
    fill_table(table, [own])
    part_ref[...] = picked_rows(spread_slots(nbr_ref[:, : part_ref.shape[0] // 8]), table)


def fine_kernel(
    par_ref, x_ref, nbr_ref, assign_ref, h1, h2, h3, h0, own_ref, edge_ref, part_ref,
    ew, nw, bias, gain, ew1,
    mid_ref, coarse_ref, sender_ref, table, near_table, sums, *, block
):
    x = x_ref[...]
    halo = []
    for axis, (first, second) in enumerate(((h0, h1), (h2, h3))):
        odd = par_ref[axis] == 1
        first, second = first[...], second[...]
        halo += [jnp.where(odd, first, second), jnp.where(odd, second, first)]
    halo = [dot(jnp.concatenate(halo, axis=0), ew[0, 1]).astype(BF16)]
    own = own_ref[...]
    fill_table(table, [own] + halo)
    fill_table(near_table, halo)
    mats, rows = level_params(ew, nw, bias, gain, edge_ref, last_weight(nw))
    rows_total = x_ref.shape[0]
    blank = rows_total + sum(piece.shape[0] for piece in halo)
    done = part_ref.shape[0] // 8
    sums[0:done] = edge_sums(
        x[0:done], nbr_ref[:, 0:done], near_table, rows_total, part_ref[...], blank, mats, rows
    )

    def step(j, carry):
        here = pl.ds(pl.multiple_of(j * block, block), block)
        nbr = nbr_ref[:, here]
        sums[here, :] = edge_sums(x_ref[here, :], nbr, table, 0, None, blank, mats, rows)
        return carry

    lax.fori_loop(done // block, rows_total // block, step, 0)
    mid = node_step(x, sums[...], mats, rows)
    mid_ref[...] = mid
    coarse = (pool(assign_ref[...], mid, coarse_ref.shape[0]) * 0.25).astype(BF16)
    coarse_ref[...] = coarse
    sender_ref[...] = dot(coarse, ew1[0, 1]).astype(BF16)


def coarse_ahead_kernel(sender_ref, nbr_ref, ew, nw, edge_ref, last_ref, part_ref, table):
    edge_ref[...] = edge_weight(ew)
    last_ref[...] = last_weight(nw)
    fill_table(table, [sender_ref])
    part_ref[...] = picked_rows(spread_slots(nbr_ref[...]), table)


def coarse_kernel(
    x_ref, nbr_ref, assign_ref, s4, s3, s2, s1, edge_ref, last_ref, part_ref,
    ew, nw, bias, gain, ew1,
    mid_ref, coarse_ref, sender_ref, table
):
    fill_table(table, [s1, s2, s3, s4])
    mats, rows = level_params(ew, nw, bias, gain, edge_ref, last_ref[...])
    x = x_ref[...]
    count = x.shape[0]
    sums = edge_sums(x, nbr_ref[...], table, count, part_ref[...], 5 * count, mats, rows)
    mid = node_step(x, sums, mats, rows)
    mid_ref[...] = mid
    coarse = (pool(assign_ref[...], mid, coarse_ref.shape[0]) * 0.25).astype(BF16)
    coarse_ref[...] = coarse
    sender_ref[...] = dot(coarse, ew1[0, 1]).astype(BF16)


def padded_nbr(nbr_ref, blank):
    extra = -nbr_ref.shape[1] % 128
    return jnp.concatenate([nbr_ref[...], jnp.full((8, extra), blank, jnp.int32)], axis=1)


def coarsest_ahead_kernel(
    sender_ref, nbr_ref, fine_assign, coarse_assign, ew, nw,
    edge_ref, last_ref, part_ref, fine_ref, coarse_ref, table, *, blank
):
    edge_ref[...] = edge_weight(ew)
    last_ref[...] = last_weight(nw)
    fill_table(table, [sender_ref])
    part_ref[...] = picked_rows(spread_slots(padded_nbr(nbr_ref, blank)), table)
    fine_ref[...] = one_hot_lanes(lane_broadcast(fine_assign[...]), fine_ref.shape[1])
    coarse_ref[...] = one_hot_lanes(lane_broadcast(coarse_assign[...]), coarse_ref.shape[1])


def coarsest_kernel(
    x_ref, nbr_ref, s2, s1, s4, s6, s3, s5, edge_ref, last_ref, part_ref, fine_hot, coarse_hot,
    ew, nw, bias, gain, fine_ref, coarse_ref, out_ref, table
):
    pieces = [s1, s2, s3, s4, s5, s6]
    fill_table(table, pieces)
    mats, rows = level_params(ew, nw, bias, gain, edge_ref, last_ref[...])
    count = x_ref.shape[0]
    blank = (len(pieces) + 1) * count
    x = jnp.concatenate([x_ref[...], jnp.zeros((-count % 128, 128), BF16)], axis=0)
    nbr = padded_nbr(nbr_ref, blank)
    sums = edge_sums(x, nbr, table, count, part_ref[...], blank, mats, rows)
    top = node_step(x, sums, mats, rows)
    coarse = (coarse_ref[...].astype(F32) + dot(coarse_hot[...], top)).astype(BF16)
    out_ref[...] = (fine_ref[...].astype(F32) + dot(fine_hot[...], coarse)).astype(BF16)


def call(kernel, operands, specs, outs, scratch, flops, name, vmem_bytes=VMEM_BYTES):
    moved = sum(o.size * o.dtype.itemsize for o in operands)
    vmem = pl.BlockSpec(memory_space=pltpu.VMEM)

    def body(*refs):
        views = [
            ref.at[pl.ds(spec, 1)] if isinstance(spec, int) else ref for ref, spec in zip(refs, specs)
        ]
        kernel(*views, *refs[len(specs) :])

    return pl.pallas_call(
        body,
        in_specs=[vmem if spec is None or isinstance(spec, int) else spec for spec in specs],
        out_specs=[vmem] * len(outs),
        out_shape=[jax.ShapeDtypeStruct(s, BF16) for s in outs],
        scratch_shapes=scratch,
        compiler_params=pltpu.CompilerParams(vmem_limit_bytes=vmem_bytes),
        cost_estimate=pl.CostEstimate(flops=flops, bytes_accessed=moved, transcendentals=0),
        name=name,
    )(*operands)


def on_device(
    node_features,
    fine_neighbors,
    send_rows,
    coarse_neighbors,
    coarsest_neighbors,
    fine_assign,
    coarse_assign,
    edge_weights,
    node_weights,
    biases,
    gains,
):
    fine_rows, width = node_features.shape
    coarse_rows = coarse_neighbors.shape[0]
    top_rows = coarsest_neighbors.shape[0]
    halo = send_rows.shape[2]
    fine_assign = fine_assign.reshape(1, -1)
    coarse_assign = coarse_assign.reshape(1, -1)
    params = [edge_weights, node_weights, biases, gains]
    wide, narrow = lax.axis_size("wide"), lax.axis_size("narrow")
    parity = jnp.stack([lax.axis_index("wide") % 2, lax.axis_index("narrow") % 2])
    smem = pl.BlockSpec(memory_space=pltpu.SMEM)

    *outgoing, rows_kept = call(
        outgoing_kernel,
        [parity, node_features, send_rows],
        [smem, None, None],
        [(halo, width)] * 4 + [(fine_rows, width)],
        [],
        8 * 2 * 4 * halo * fine_rows * width,
        "outgoing",
    )
    block = 512
    ahead = 1 * block
    table = functools.partial(pltpu.VMEM, dtype=BF16)
    weights = [(2 * width, 2 * width), (width, width)]
    odd_pairs = [(i, (i + 1) % wide) for i in range(1, wide, 2)]
    even_pairs = [(i, i + 1) for i in range(0, wide, 2)]
    odd_narrow = [(i, (i + 1) % narrow) for i in range(1, narrow, 2)]
    even_narrow = [(i, i + 1) for i in range(0, narrow, 2)]
    from_odd = exchange(outgoing[1], "wide", odd_pairs)
    from_even_n = exchange(outgoing[2], "narrow", even_narrow)
    from_odd_n = exchange(outgoing[3], "narrow", odd_narrow)
    from_even = exchange(outgoing[0], "wide", even_pairs)
    fine_ahead = call(
        fine_ahead_kernel,
        [rows_kept, fine_neighbors.T, edge_weights],
        [None, None, 0],
        [(fine_rows, width), weights[0], (8 * ahead, width)],
        [table((fine_rows // 2, 2 * width))],
        2 * 8 * ahead * fine_rows * width,
        "fine_ahead",
    )
    fine_mid, coarse_in, sender = call(
        functools.partial(fine_kernel, block=block),
        [parity, rows_kept, fine_neighbors.T, fine_assign]
        + [from_odd, from_even_n, from_odd_n, from_even]
        + list(fine_ahead)
        + params
        + [edge_weights],
        [smem] + [None] * 10 + [0, 0, 0, 0, 1],
        [(fine_rows, width), (coarse_rows, width), (coarse_rows, width)],
        [
            table(((fine_rows + 4 * halo) // 2, 2 * width)),
            table((2 * halo, 2 * width)),
            table((fine_rows, width)),
        ],
        2 * 8 * fine_rows * (fine_rows + 4 * halo) * width,
        "fine_level",
    )
    far_n = from_partner(sender, "narrow", 1)
    near_n = from_partner(sender, "narrow", 0)
    far_w = from_partner(sender, "wide", 1)
    near_w = from_partner(sender, "wide", 0)
    coarse_ahead = call(
        coarse_ahead_kernel,
        [sender, coarse_neighbors.T, edge_weights, node_weights],
        [None, None, 1, 1],
        weights + [(8 * coarse_rows, width)],
        [table((-(-coarse_rows // 256) * 128, 2 * width))],
        2 * 8 * coarse_rows * coarse_rows * width,
        "coarse_ahead",
    )
    coarse_mid, top_in, sender = call(
        coarse_kernel,
        [coarse_in, coarse_neighbors.T, coarse_assign, far_n, near_n, far_w, near_w]
        + list(coarse_ahead)
        + params
        + [edge_weights],
        [None] * 10 + [1, 1, 1, 1, 2],
        [(coarse_rows, width), (top_rows, width), (top_rows, width)],
        [table((-(-4 * coarse_rows // 256) * 128, 2 * width))],
        2 * 8 * coarse_rows * 4 * coarse_rows * width,
        "coarse_level",
    )
    wide_bits = wide.bit_length() - 1
    arrived = [from_partner(sender, "wide", bit) for bit in (1, 0, 3, 5, 2, 4)]
    top_pad = -(-top_rows // 128) * 128
    coarsest_ahead = call(
        functools.partial(coarsest_ahead_kernel, blank=(wide_bits + 1) * top_rows),
        [sender, coarsest_neighbors.T, fine_assign, coarse_assign, edge_weights, node_weights],
        [None] * 4 + [2, 2],
        weights + [(8 * top_pad, width), (fine_rows, coarse_rows), (coarse_rows, top_pad)],
        [table((128, 2 * width))],
        2 * fine_rows * coarse_rows * width,
        "coarsest_ahead",
    )
    (result,) = call(
        coarsest_kernel,
        [top_in, coarsest_neighbors.T]
        + arrived
        + list(coarsest_ahead)
        + params
        + [fine_mid, coarse_mid],
        [None] * 13 + [2, 2, 2, 2] + [None] * 2,
        [(fine_rows, width)],
        [table((-(-wide_bits * top_rows // 256) * 128, 2 * width))],
        2 * fine_rows * coarse_rows * width,
        "coarsest_level",
    )
    return result


def solution(mesh):
    rows = P(("wide", "narrow"), None)
    flat = P(("wide", "narrow"))
    in_specs = (rows, rows, P(("wide", "narrow"), None, None), rows, rows, flat, flat) + (P(),) * 4
    return jax.shard_map(
        on_device, mesh=mesh, in_specs=in_specs, out_specs=rows, check_vma=False
    )
```

```python
import functools

import jax
import jax.numpy as jnp
from jax import lax
from jax.experimental import pallas as pl
from jax.experimental.pallas import tpu as pltpu
from jax.sharding import PartitionSpec as P

F32 = jnp.float32
BF16 = jnp.bfloat16
I16 = jnp.int16
VMEM_BYTES = 24 * 1024 * 1024


def exchange(block, axis, pairs):
    route = [(i, j) for i, j in pairs] + [(j, i) for i, j in pairs]
    return lax.ppermute(block, axis, route)


def from_partner(block, axis, apart):
    count = lax.axis_size(axis)
    return lax.ppermute(block, axis, [(i, i ^ apart) for i in range(count)])


def dot(a, b):
    return jnp.dot(a, b, preferred_element_type=F32)


def one_hot(column, width):
    lanes = lax.broadcasted_iota(jnp.int32, (column.shape[0], width), 1)
    return (column == lanes).astype(BF16)


def centred_columns(matrix):
    wide = matrix.astype(F32)
    return wide - jnp.mean(wide, axis=-1, keepdims=True)


def block_diag(matrix):
    zero = jnp.zeros_like(matrix)
    return jnp.concatenate(
        [jnp.concatenate([matrix, zero], axis=1), jnp.concatenate([zero, matrix], axis=1)], axis=0
    )


def fill_table(table, pieces):
    half = table.shape[0]
    start = 0
    for piece in pieces:
        rows = piece.shape[0]
        cut = min(rows, max(0, half - start))
        if cut > 0:
            table[start : start + cut, 0:128] = piece[0:cut]
        if cut < rows:
            low = start + cut - half
            table[low : low + rows - cut, 128:256] = piece[cut:rows]
        start += rows
    if start < half:
        table[start:half, 0:128] = jnp.zeros((half - start, 128), BF16)
    gap = max(start - half, 0)
    if gap < half:
        table[gap:half, 128:256] = jnp.zeros((half - gap, 128), BF16)


def lane_broadcast(row):
    tiles = [
        jnp.broadcast_to(row[:, b : b + 128], (128, 128)).astype(I16).T
        for b in range(0, row.shape[1], 128)
    ]
    return jnp.concatenate(tiles, axis=0) if len(tiles) > 1 else tiles[0]


def one_hot_lanes(code, width):
    parts = []
    for start in range(0, width, 128):
        lanes = lax.broadcasted_iota(I16, code.shape, 1) + I16(start)
        parts.append(jnp.where(code == lanes, BF16(1), BF16(0)))
    return jnp.concatenate(parts, axis=1)


def spread_slots(nbr):
    return jnp.concatenate([lane_broadcast(nbr[k : k + 1]) for k in range(nbr.shape[0])], axis=0)


def picked_rows(code, table):
    half = table.shape[0]
    high = code >= I16(half)
    low = jnp.where(high, code - I16(half), code)
    got = dot(one_hot_lanes(low, half), table[...]).astype(BF16)
    return jnp.where(high, got[:, 128:256], got[:, 0:128])


def unit_rows(c):
    return c * lax.rsqrt(jnp.mean(c * c, axis=-1, keepdims=True) + 1e-5)


def edge_sums(x, nbr, table, first, partial, blank, mats, rows):
    w_recv, w_out2 = mats[:2]
    b_hid, b_out2, gain_e, empty = rows[:4]
    block = x.shape[0]
    slots = nbr.shape[0]
    receive = dot(x, w_recv) + b_hid
    code = spread_slots(nbr)
    sent = picked_rows(code - I16(first) if first else code, table)
    if partial is not None:
        sent = sent + partial
    sent = sent.astype(F32)
    hid = jnp.maximum(jnp.concatenate([receive] * slots, axis=0) + sent, 0.0).astype(BF16)
    hid = jnp.where(code < I16(blank), hid, BF16(0))
    split = slots // 2 * block
    c = dot(jnp.concatenate([hid[:split], hid[split:]], axis=1), w_out2) + b_out2
    m = unit_rows(c[:, 0:128]) + unit_rows(c[:, 128:256])
    total = m[0:block]
    for k in range(1, slots // 2):
        total = total + m[k * block : (k + 1) * block]
    missing = jnp.sum((nbr >= blank).astype(F32), axis=0, keepdims=True)
    missing = jnp.broadcast_to(missing, (8, block)).T[:, 0:1]
    return ((total - missing * empty) * gain_e).astype(BF16)


def node_step(x, summed, mats, rows):
    w_node, w_last = mats[2:]
    b_node, b_last, gain_n = rows[4:]
    upd = jnp.maximum(dot(jnp.concatenate([x, summed], axis=1), w_node) + b_node, 0.0).astype(BF16)
    return (x.astype(F32) + unit_rows(dot(upd, w_last) + b_last) * gain_n).astype(BF16)


def edge_weight(ew):
    return block_diag(centred_columns(ew[0, 2]).astype(BF16))


def last_weight(nw):
    return centred_columns(nw[0, 2]).astype(BF16)


def level_params(ew, nw, bias, gain, w_out2, w_last):
    w_node = jnp.concatenate([nw[0, 0], nw[0, 1]], axis=0)
    mats = (ew[0, 0], w_out2[...], w_node, w_last)
    b = bias[0]
    b_out = b[1:2] - jnp.mean(b[1:2])
    b_last = b[3:4] - jnp.mean(b[3:4])
    g = gain[0]
    b_pair = jnp.concatenate([b_out, b_out], axis=1)
    rows = (b[0:1], b_pair, g[0:1], unit_rows(b_out), b[2:3], b_last, g[1:2])
    return mats, rows


def membership(assign, groups):
    rows = assign.shape[1]
    group = lax.broadcasted_iota(I16, (groups, rows), 0)
    spread = jnp.broadcast_to(assign, (groups, rows)).astype(I16)
    return jnp.where(group == spread, BF16(1), BF16(0))


def outgoing_kernel(par_ref, x_ref, send_ref, *out_refs):
    lists = []
    for axis in range(2):
        odd = par_ref[axis] == 1
        up, down = send_ref[0, 2 * axis : 2 * axis + 1], send_ref[0, 2 * axis + 1 : 2 * axis + 2]
        lists += [jnp.where(odd, down, up), jnp.where(odd, up, down)]
    code = lane_broadcast(jnp.concatenate(lists, axis=1))
    x = x_ref[...]
    out_refs[4][...] = x
    half = x.shape[0] // 2
    high = code >= I16(half)
    low = jnp.where(high, code - I16(half), code)
    pair = jnp.concatenate([x[:half], x[half:]], axis=1)
    got = dot(one_hot_lanes(low, half), pair).astype(BF16)
    got = jnp.where(high, got[:, 128:256], got[:, 0:128])
    rows = out_refs[0].shape[0]
    for k, out in enumerate(out_refs[:4]):
        out[...] = got[k * rows : (k + 1) * rows]


def fine_ahead_kernel(
    x_ref, nbr_ref, assign_ref, ew, own_ref, edge_ref, part_ref, member_ref, table
):
    own = dot(x_ref[...], ew[0, 1]).astype(BF16)
    own_ref[...] = own
    edge_ref[...] = edge_weight(ew)
    fill_table(table, [own])
    part_ref[...] = picked_rows(spread_slots(nbr_ref[:, : part_ref.shape[0] // 8]), table)
    member_ref[...] = membership(assign_ref[...], member_ref.shape[0])


def fine_kernel(
    par_ref, x_ref, nbr_ref, h1, h2, h3, h0, own_ref, edge_ref, part_ref, member_ref,
    ew, nw, bias, gain, ew1,
    mid_ref, coarse_ref, sender_ref, table, near_table, sums, *, block
):
    x = x_ref[...]
    halo = []
    for axis, (first, second) in enumerate(((h0, h1), (h2, h3))):
        odd = par_ref[axis] == 1
        first, second = first[...], second[...]
        halo += [jnp.where(odd, first, second), jnp.where(odd, second, first)]
    halo = [dot(jnp.concatenate(halo, axis=0), ew[0, 1]).astype(BF16)]
    own = own_ref[...]
    fill_table(table, [own] + halo)
    fill_table(near_table, halo)
    mats, rows = level_params(ew, nw, bias, gain, edge_ref, last_weight(nw))
    rows_total = x_ref.shape[0]
    blank = rows_total + sum(piece.shape[0] for piece in halo)
    done = part_ref.shape[0] // 8
    sums[0:done] = edge_sums(
        x[0:done], nbr_ref[:, 0:done], near_table, rows_total, part_ref[...], blank, mats, rows
    )

    def step(j, carry):
        here = pl.ds(pl.multiple_of(j * block, block), block)
        nbr = nbr_ref[:, here]
        sums[here, :] = edge_sums(x_ref[here, :], nbr, table, 0, None, blank, mats, rows)
        return carry

    lax.fori_loop(done // block, rows_total // block, step, 0)
    mid = node_step(x, sums[...], mats, rows)
    mid_ref[...] = mid
    coarse = (dot(member_ref[...], mid) * 0.25).astype(BF16)
    coarse_ref[...] = coarse
    sender_ref[...] = dot(coarse, ew1[0, 1]).astype(BF16)


def coarse_ahead_kernel(
    sender_ref, nbr_ref, fine_assign, coarse_assign, ew, nw,
    edge_ref, last_ref, part_ref, fine_hot, top_hot, table
):
    hot = one_hot_lanes(lane_broadcast(fine_assign[...]), fine_hot.shape[1])
    fine_hot[...] = hot
    coarse_hot = one_hot_lanes(lane_broadcast(coarse_assign[...]), top_hot.shape[1])
    top_hot[...] = dot(hot, coarse_hot).astype(BF16)
    edge_ref[...] = edge_weight(ew)
    last_ref[...] = last_weight(nw)
    fill_table(table, [sender_ref])
    part_ref[...] = picked_rows(spread_slots(nbr_ref[...]), table)


def coarse_kernel(
    x_ref, nbr_ref, assign_ref, s4, s3, s2, s1, edge_ref, last_ref, part_ref,
    ew, nw, bias, gain, ew1,
    mid_ref, coarse_ref, sender_ref, table
):
    fill_table(table, [s1, s2, s3, s4])
    mats, rows = level_params(ew, nw, bias, gain, edge_ref, last_ref[...])
    x = x_ref[...]
    count = x.shape[0]
    sums = edge_sums(x, nbr_ref[...], table, count, part_ref[...], 5 * count, mats, rows)
    mid = node_step(x, sums, mats, rows)
    mid_ref[...] = mid
    coarse = (dot(membership(assign_ref[...], coarse_ref.shape[0]), mid) * 0.25).astype(BF16)
    coarse_ref[...] = coarse
    sender_ref[...] = dot(coarse, ew1[0, 1]).astype(BF16)


def padded_nbr(nbr_ref, blank):
    extra = -nbr_ref.shape[1] % 128
    return jnp.concatenate([nbr_ref[...], jnp.full((8, extra), blank, jnp.int32)], axis=1)


def coarsest_ahead_kernel(
    sender_ref, nbr_ref, fine_hot, fine_ref, coarse_ref, ew, nw,
    edge_ref, last_ref, part_ref, base_ref, table, *, blank
):
    edge_ref[...] = edge_weight(ew)
    last_ref[...] = last_weight(nw)
    fill_table(table, [sender_ref])
    part_ref[...] = picked_rows(spread_slots(padded_nbr(nbr_ref, blank)), table)
    base_ref[...] = fine_ref[...].astype(F32) + dot(fine_hot[...], coarse_ref[...])


def coarsest_kernel(
    x_ref, nbr_ref, s2, s1, s3, s5, s4, s6, edge_ref, last_ref, part_ref, base_ref, top_hot,
    ew, nw, bias, gain, out_ref, table
):
    pieces = [s1, s2, s3, s4, s5, s6]
    fill_table(table, pieces)
    mats, rows = level_params(ew, nw, bias, gain, edge_ref, last_ref[...])
    count = x_ref.shape[0]
    blank = (len(pieces) + 1) * count
    x = jnp.concatenate([x_ref[...], jnp.zeros((-count % 128, 128), BF16)], axis=0)
    nbr = padded_nbr(nbr_ref, blank)
    sums = edge_sums(x, nbr, table, count, part_ref[...], blank, mats, rows)
    top = node_step(x, sums, mats, rows)
    out_ref[...] = (base_ref[...] + dot(top_hot[...], top)).astype(BF16)


def call(kernel, operands, specs, outs, scratch, flops, name, vmem_bytes=VMEM_BYTES):
    moved = sum(o.size * o.dtype.itemsize for o in operands)
    vmem = pl.BlockSpec(memory_space=pltpu.VMEM)

    def body(*refs):
        views = [
            ref.at[pl.ds(spec, 1)] if isinstance(spec, int) else ref for ref, spec in zip(refs, specs)
        ]
        kernel(*views, *refs[len(specs) :])

    return pl.pallas_call(
        body,
        in_specs=[vmem if spec is None or isinstance(spec, int) else spec for spec in specs],
        out_specs=[vmem] * len(outs),
        out_shape=[o if hasattr(o, "dtype") else jax.ShapeDtypeStruct(o, BF16) for o in outs],
        scratch_shapes=scratch,
        compiler_params=pltpu.CompilerParams(vmem_limit_bytes=vmem_bytes),
        cost_estimate=pl.CostEstimate(flops=flops, bytes_accessed=moved, transcendentals=0),
        name=name,
    )(*operands)


def on_device(
    node_features,
    fine_neighbors,
    send_rows,
    coarse_neighbors,
    coarsest_neighbors,
    fine_assign,
    coarse_assign,
    edge_weights,
    node_weights,
    biases,
    gains,
):
    fine_rows, width = node_features.shape
    coarse_rows = coarse_neighbors.shape[0]
    top_rows = coarsest_neighbors.shape[0]
    halo = send_rows.shape[2]
    fine_assign = fine_assign.reshape(1, -1)
    coarse_assign = coarse_assign.reshape(1, -1)
    params = [edge_weights, node_weights, biases, gains]
    wide, narrow = lax.axis_size("wide"), lax.axis_size("narrow")
    parity = jnp.stack([lax.axis_index("wide") % 2, lax.axis_index("narrow") % 2])
    smem = pl.BlockSpec(memory_space=pltpu.SMEM)

    *outgoing, rows_kept = call(
        outgoing_kernel,
        [parity, node_features, send_rows],
        [smem, None, None],
        [(halo, width)] * 4 + [(fine_rows, width)],
        [],
        8 * 2 * 4 * halo * fine_rows * width,
        "outgoing",
    )
    block = 512
    ahead = 1 * block
    table = functools.partial(pltpu.VMEM, dtype=BF16)
    weights = [(2 * width, 2 * width), (width, width)]
    odd_pairs = [(i, (i + 1) % wide) for i in range(1, wide, 2)]
    even_pairs = [(i, i + 1) for i in range(0, wide, 2)]
    odd_narrow = [(i, (i + 1) % narrow) for i in range(1, narrow, 2)]
    even_narrow = [(i, i + 1) for i in range(0, narrow, 2)]
    from_odd = exchange(outgoing[1], "wide", odd_pairs)
    from_even_n = exchange(outgoing[2], "narrow", even_narrow)
    from_odd_n = exchange(outgoing[3], "narrow", odd_narrow)
    from_even = exchange(outgoing[0], "wide", even_pairs)
    fine_ahead = call(
        fine_ahead_kernel,
        [rows_kept, fine_neighbors.T, fine_assign, edge_weights],
        [None, None, None, 0],
        [(fine_rows, width), weights[0], (8 * ahead, width), (coarse_rows, fine_rows)],
        [table((fine_rows // 2, 2 * width))],
        2 * 8 * ahead * fine_rows * width,
        "fine_ahead",
    )
    fine_mid, coarse_in, sender = call(
        functools.partial(fine_kernel, block=block),
        [parity, rows_kept, fine_neighbors.T]
        + [from_odd, from_even_n, from_odd_n, from_even]
        + list(fine_ahead)
        + params
        + [edge_weights],
        [smem] + [None] * 10 + [0, 0, 0, 0, 1],
        [(fine_rows, width), (coarse_rows, width), (coarse_rows, width)],
        [
            table(((fine_rows + 4 * halo) // 2, 2 * width)),
            table((2 * halo, 2 * width)),
            table((fine_rows, width)),
        ],
        2 * 8 * fine_rows * (fine_rows + 4 * halo) * width,
        "fine_level",
    )
    far_n = from_partner(sender, "narrow", 2)
    near_n = from_partner(sender, "narrow", 1)
    far_w = from_partner(sender, "wide", 2)
    near_w = from_partner(sender, "wide", 1)
    top_pad = -(-top_rows // 128) * 128
    *coarse_ahead, fine_hot, top_hot = call(
        coarse_ahead_kernel,
        [sender, coarse_neighbors.T, fine_assign, coarse_assign, edge_weights, node_weights],
        [None, None, None, None, 1, 1],
        weights + [(8 * coarse_rows, width), (fine_rows, coarse_rows), (fine_rows, top_pad)],
        [table((-(-coarse_rows // 256) * 128, 2 * width))],
        2 * 8 * coarse_rows * coarse_rows * width,
        "coarse_ahead",
    )
    coarse_mid, top_in, sender = call(
        coarse_kernel,
        [coarse_in, coarse_neighbors.T, coarse_assign, far_n, near_n, far_w, near_w]
        + list(coarse_ahead)
        + params
        + [edge_weights],
        [None] * 10 + [1, 1, 1, 1, 2],
        [(coarse_rows, width), (top_rows, width), (top_rows, width)],
        [table((-(-4 * coarse_rows // 256) * 128, 2 * width))],
        2 * 8 * coarse_rows * 4 * coarse_rows * width,
        "coarse_level",
    )
    wide_bits = wide.bit_length() - 1
    arrived = [from_partner(sender, "wide", 1 << bit) for bit in range(wide_bits)]
    arrived[3] = from_partner(arrived[2], "wide", 12)
    arrived[5] = from_partner(arrived[4], "wide", 48)
    arrived = [arrived[bit] for bit in (1, 0, 2, 4, 3, 5)]
    coarsest_ahead = call(
        functools.partial(coarsest_ahead_kernel, blank=(wide_bits + 1) * top_rows),
        [sender, coarsest_neighbors.T, fine_hot, fine_mid, coarse_mid]
        + [edge_weights, node_weights],
        [None] * 5 + [2, 2],
        weights + [(8 * top_pad, width), jax.ShapeDtypeStruct((fine_rows, width), F32)],
        [table((128, 2 * width))],
        2 * fine_rows * coarse_rows * width,
        "coarsest_ahead",
    )
    (result,) = call(
        coarsest_kernel,
        [top_in, coarsest_neighbors.T]
        + arrived
        + list(coarsest_ahead)
        + [top_hot]
        + params,
        [None] * 13 + [2, 2, 2, 2],
        [(fine_rows, width)],
        [table((-(-wide_bits * top_rows // 256) * 128, 2 * width))],
        2 * fine_rows * coarse_rows * width,
        "coarsest_level",
    )
    return result


def solution(mesh):
    rows = P(("wide", "narrow"), None)
    flat = P(("wide", "narrow"))
    in_specs = (rows, rows, P(("wide", "narrow"), None, None), rows, rows, flat, flat) + (P(),) * 4
    return jax.shard_map(
        on_device, mesh=mesh, in_specs=in_specs, out_specs=rows, check_vma=False
    )
```

```python
import functools

import jax
import jax.numpy as jnp
from jax import lax
from jax.experimental import pallas as pl
from jax.experimental.pallas import tpu as pltpu
from jax.sharding import PartitionSpec as P

F32 = jnp.float32
BF16 = jnp.bfloat16
I16 = jnp.int16
VMEM_BYTES = 24 * 1024 * 1024


def exchange(block, axis, pairs):
    route = [(i, j) for i, j in pairs] + [(j, i) for i, j in pairs]
    return lax.ppermute(block, axis, route)


def from_partner(block, axis, apart):
    count = lax.axis_size(axis)
    return lax.ppermute(block, axis, [(i, i ^ apart) for i in range(count)])


def dot(a, b):
    return jnp.dot(a, b, preferred_element_type=F32)


def one_hot(column, width):
    lanes = lax.broadcasted_iota(jnp.int32, (column.shape[0], width), 1)
    return (column == lanes).astype(BF16)


def centred_columns(matrix):
    wide = matrix.astype(F32)
    return wide - jnp.mean(wide, axis=-1, keepdims=True)


def block_diag(matrix):
    zero = jnp.zeros_like(matrix)
    return jnp.concatenate(
        [jnp.concatenate([matrix, zero], axis=1), jnp.concatenate([zero, matrix], axis=1)], axis=0
    )


def fill_table(table, pieces):
    half = table.shape[0]
    start = 0
    for piece in pieces:
        rows = piece.shape[0]
        cut = min(rows, max(0, half - start))
        if cut > 0:
            table[start : start + cut, 0:128] = piece[0:cut]
        if cut < rows:
            low = start + cut - half
            table[low : low + rows - cut, 128:256] = piece[cut:rows]
        start += rows
    if start < half:
        table[start:half, 0:128] = jnp.zeros((half - start, 128), BF16)
    gap = max(start - half, 0)
    if gap < half:
        table[gap:half, 128:256] = jnp.zeros((half - gap, 128), BF16)


def lane_broadcast(row):
    tiles = [
        jnp.broadcast_to(row[:, b : b + 128], (128, 128)).astype(I16).T
        for b in range(0, row.shape[1], 128)
    ]
    return jnp.concatenate(tiles, axis=0) if len(tiles) > 1 else tiles[0]


def one_hot_lanes(code, width):
    parts = []
    for start in range(0, width, 128):
        lanes = lax.broadcasted_iota(I16, code.shape, 1) + I16(start)
        parts.append(jnp.where(code == lanes, BF16(1), BF16(0)))
    return jnp.concatenate(parts, axis=1)


def spread_slots(nbr):
    return jnp.concatenate([lane_broadcast(nbr[k : k + 1]) for k in range(nbr.shape[0])], axis=0)


def picked_rows(code, table):
    half = table.shape[0]
    high = code >= I16(half)
    low = jnp.where(high, code - I16(half), code)
    got = dot(one_hot_lanes(low, half), table[...]).astype(BF16)
    return jnp.where(high, got[:, 128:256], got[:, 0:128])


def unit_rows(c):
    return c * lax.rsqrt(jnp.mean(c * c, axis=-1, keepdims=True) + 1e-5)


def edge_sums(x, nbr, table, first, partial, blank, mats, rows):
    w_recv, w_out2 = mats[:2]
    b_hid, b_out2, gain_e, empty = rows[:4]
    block = x.shape[0]
    slots = nbr.shape[0]
    receive = dot(x, w_recv) + b_hid
    code = spread_slots(nbr)
    sent = picked_rows(code - I16(first) if first else code, table)
    if partial is not None:
        sent = sent + partial
    sent = sent.astype(F32)
    hid = jnp.maximum(jnp.concatenate([receive] * slots, axis=0) + sent, 0.0).astype(BF16)
    hid = jnp.where(code < I16(blank), hid, BF16(0))
    split = slots // 2 * block
    c = dot(jnp.concatenate([hid[:split], hid[split:]], axis=1), w_out2) + b_out2
    m = unit_rows(c[:, 0:128]) + unit_rows(c[:, 128:256])
    total = m[0:block]
    for k in range(1, slots // 2):
        total = total + m[k * block : (k + 1) * block]
    missing = jnp.sum((nbr >= blank).astype(F32), axis=0, keepdims=True)
    missing = jnp.broadcast_to(missing, (8, block)).T[:, 0:1]
    return ((total - missing * empty) * gain_e).astype(BF16)


def node_step(x, summed, mats, rows):
    w_node, w_last = mats[2:]
    b_node, b_last, gain_n = rows[4:]
    upd = jnp.maximum(dot(jnp.concatenate([x, summed], axis=1), w_node) + b_node, 0.0).astype(BF16)
    return (x.astype(F32) + unit_rows(dot(upd, w_last) + b_last) * gain_n).astype(BF16)


def edge_weight(ew):
    return block_diag(centred_columns(ew[0, 2]).astype(BF16))


def last_weight(nw):
    return centred_columns(nw[0, 2]).astype(BF16)


def level_params(ew, nw, bias, gain, w_out2, w_last):
    w_node = jnp.concatenate([nw[0, 0], nw[0, 1]], axis=0)
    mats = (ew[0, 0], w_out2[...], w_node, w_last)
    b = bias[0]
    b_out = b[1:2] - jnp.mean(b[1:2])
    b_last = b[3:4] - jnp.mean(b[3:4])
    g = gain[0]
    b_pair = jnp.concatenate([b_out, b_out], axis=1)
    rows = (b[0:1], b_pair, g[0:1], unit_rows(b_out), b[2:3], b_last, g[1:2])
    return mats, rows


def membership(assign, groups):
    rows = assign.shape[1]
    group = lax.broadcasted_iota(I16, (groups, rows), 0)
    spread = jnp.broadcast_to(assign, (groups, rows)).astype(I16)
    return jnp.where(group == spread, BF16(1), BF16(0))


def listed_kernel(par_ref, send_ref, hot_ref, code_ref):
    lists = []
    for axis in range(2):
        odd = par_ref[axis] == 1
        up, down = send_ref[0, 2 * axis : 2 * axis + 1], send_ref[0, 2 * axis + 1 : 2 * axis + 2]
        lists += [jnp.where(odd, down, up), jnp.where(odd, up, down)]
    code = lane_broadcast(jnp.concatenate(lists, axis=1))
    code_ref[...] = code
    half = hot_ref.shape[1]
    hot_ref[...] = one_hot_lanes(jnp.where(code >= I16(half), code - I16(half), code), half)


def outgoing_kernel(x_ref, hot_ref, code_ref, *out_refs):
    x = x_ref[...]
    out_refs[4][...] = x
    half = x.shape[0] // 2
    pair = jnp.concatenate([x[:half], x[half:]], axis=1)
    got = dot(hot_ref[...], pair).astype(BF16)
    got = jnp.where(code_ref[...] >= I16(half), got[:, 128:256], got[:, 0:128])
    rows = out_refs[0].shape[0]
    for k, out in enumerate(out_refs[:4]):
        out[...] = got[k * rows : (k + 1) * rows]


def fine_ahead_kernel(
    x_ref, nbr_ref, assign_ref, ew, own_ref, edge_ref, part_ref, member_ref, table
):
    own = dot(x_ref[...], ew[0, 1]).astype(BF16)
    own_ref[...] = own
    edge_ref[...] = edge_weight(ew)
    fill_table(table, [own])
    part_ref[...] = picked_rows(spread_slots(nbr_ref[:, : part_ref.shape[0] // 8]), table)
    member_ref[...] = membership(assign_ref[...], member_ref.shape[0])


def fine_kernel(
    par_ref, x_ref, nbr_ref, h1, h2, h3, h0, own_ref, edge_ref, part_ref, member_ref,
    ew, nw, bias, gain, ew1,
    mid_ref, coarse_ref, sender_ref, table, near_table, sums, *, block
):
    x = x_ref[...]
    halo = []
    for axis, (first, second) in enumerate(((h0, h1), (h2, h3))):
        odd = par_ref[axis] == 1
        first, second = first[...], second[...]
        halo += [jnp.where(odd, first, second), jnp.where(odd, second, first)]
    halo = [dot(jnp.concatenate(halo, axis=0), ew[0, 1]).astype(BF16)]
    own = own_ref[...]
    fill_table(table, [own] + halo)
    fill_table(near_table, halo)
    mats, rows = level_params(ew, nw, bias, gain, edge_ref, last_weight(nw))
    rows_total = x_ref.shape[0]
    blank = rows_total + sum(piece.shape[0] for piece in halo)
    done = part_ref.shape[0] // 8
    sums[0:done] = edge_sums(
        x[0:done], nbr_ref[:, 0:done], near_table, rows_total, part_ref[...], blank, mats, rows
    )

    def step(j, carry):
        here = pl.ds(pl.multiple_of(j * block, block), block)
        nbr = nbr_ref[:, here]
        sums[here, :] = edge_sums(x_ref[here, :], nbr, table, 0, None, blank, mats, rows)
        return carry

    lax.fori_loop(done // block, rows_total // block, step, 0)
    mid = node_step(x, sums[...], mats, rows)
    mid_ref[...] = mid
    coarse = (dot(member_ref[...], mid) * 0.25).astype(BF16)
    coarse_ref[...] = coarse
    sender_ref[...] = dot(coarse, ew1[0, 1]).astype(BF16)


def coarse_ahead_kernel(
    sender_ref, nbr_ref, fine_assign, coarse_assign, ew, nw,
    edge_ref, last_ref, part_ref, fine_hot, top_hot, table
):
    hot = one_hot_lanes(lane_broadcast(fine_assign[...]), fine_hot.shape[1])
    fine_hot[...] = hot
    coarse_hot = one_hot_lanes(lane_broadcast(coarse_assign[...]), top_hot.shape[1])
    top_hot[...] = dot(hot, coarse_hot).astype(BF16)
    edge_ref[...] = edge_weight(ew)
    last_ref[...] = last_weight(nw)
    fill_table(table, [sender_ref])
    part_ref[...] = picked_rows(spread_slots(nbr_ref[...]), table)


def coarse_kernel(
    x_ref, nbr_ref, assign_ref, s4, s3, s2, s1, edge_ref, last_ref, part_ref,
    ew, nw, bias, gain, ew1,
    mid_ref, coarse_ref, sender_ref, table
):
    fill_table(table, [s1, s2, s3, s4])
    mats, rows = level_params(ew, nw, bias, gain, edge_ref, last_ref[...])
    x = x_ref[...]
    count = x.shape[0]
    sums = edge_sums(x, nbr_ref[...], table, count, part_ref[...], 5 * count, mats, rows)
    mid = node_step(x, sums, mats, rows)
    mid_ref[...] = mid
    coarse = (dot(membership(assign_ref[...], coarse_ref.shape[0]), mid) * 0.25).astype(BF16)
    coarse_ref[...] = coarse
    sender_ref[...] = dot(coarse, ew1[0, 1]).astype(BF16)


def padded_nbr(nbr_ref, blank):
    extra = -nbr_ref.shape[1] % 128
    return jnp.concatenate([nbr_ref[...], jnp.full((8, extra), blank, jnp.int32)], axis=1)


def coarsest_ahead_kernel(
    sender_ref, nbr_ref, fine_hot, fine_ref, coarse_ref, ew, nw,
    edge_ref, last_ref, part_ref, base_ref, table, *, blank
):
    edge_ref[...] = edge_weight(ew)
    last_ref[...] = last_weight(nw)
    fill_table(table, [sender_ref])
    part_ref[...] = picked_rows(spread_slots(padded_nbr(nbr_ref, blank)), table)
    base_ref[...] = fine_ref[...].astype(F32) + dot(fine_hot[...], coarse_ref[...])


def coarsest_kernel(
    x_ref, nbr_ref, s2, s1, s3, s5, s4, s6, edge_ref, last_ref, part_ref, base_ref, top_hot,
    ew, nw, bias, gain, out_ref, table
):
    pieces = [s1, s2, s3, s4, s5, s6]
    fill_table(table, pieces)
    mats, rows = level_params(ew, nw, bias, gain, edge_ref, last_ref[...])
    count = x_ref.shape[0]
    blank = (len(pieces) + 1) * count
    x = jnp.concatenate([x_ref[...], jnp.zeros((-count % 128, 128), BF16)], axis=0)
    nbr = padded_nbr(nbr_ref, blank)
    sums = edge_sums(x, nbr, table, count, part_ref[...], blank, mats, rows)
    top = node_step(x, sums, mats, rows)
    out_ref[...] = (base_ref[...] + dot(top_hot[...], top)).astype(BF16)


def call(kernel, operands, specs, outs, scratch, flops, name, vmem_bytes=VMEM_BYTES):
    moved = sum(o.size * o.dtype.itemsize for o in operands)
    vmem = pl.BlockSpec(memory_space=pltpu.VMEM)

    def body(*refs):
        views = [
            ref.at[pl.ds(spec, 1)] if isinstance(spec, int) else ref for ref, spec in zip(refs, specs)
        ]
        kernel(*views, *refs[len(specs) :])

    return pl.pallas_call(
        body,
        in_specs=[vmem if spec is None or isinstance(spec, int) else spec for spec in specs],
        out_specs=[vmem] * len(outs),
        out_shape=[o if hasattr(o, "dtype") else jax.ShapeDtypeStruct(o, BF16) for o in outs],
        scratch_shapes=scratch,
        compiler_params=pltpu.CompilerParams(vmem_limit_bytes=vmem_bytes),
        cost_estimate=pl.CostEstimate(flops=flops, bytes_accessed=moved, transcendentals=0),
        name=name,
    )(*operands)


def on_device(
    node_features,
    fine_neighbors,
    send_rows,
    coarse_neighbors,
    coarsest_neighbors,
    fine_assign,
    coarse_assign,
    edge_weights,
    node_weights,
    biases,
    gains,
):
    fine_rows, width = node_features.shape
    coarse_rows = coarse_neighbors.shape[0]
    top_rows = coarsest_neighbors.shape[0]
    halo = send_rows.shape[2]
    fine_assign = fine_assign.reshape(1, -1)
    coarse_assign = coarse_assign.reshape(1, -1)
    params = [edge_weights, node_weights, biases, gains]
    wide, narrow = lax.axis_size("wide"), lax.axis_size("narrow")
    parity = jnp.stack([lax.axis_index("wide") % 2, lax.axis_index("narrow") % 2])
    smem = pl.BlockSpec(memory_space=pltpu.SMEM)

    listed = call(
        listed_kernel,
        [parity, send_rows],
        [smem, None],
        [(4 * halo, fine_rows // 2), jax.ShapeDtypeStruct((4 * halo, width), I16)],
        [],
        8 * 4 * halo * fine_rows * width,
        "listed",
    )
    *outgoing, rows_kept = call(
        outgoing_kernel,
        [node_features] + list(listed),
        [None, None, None],
        [(halo, width)] * 4 + [(fine_rows, width)],
        [],
        8 * 2 * 4 * halo * fine_rows * width,
        "outgoing",
    )
    block = 512
    ahead = 1 * block
    table = functools.partial(pltpu.VMEM, dtype=BF16)
    weights = [(2 * width, 2 * width), (width, width)]
    odd_pairs = [(i, (i + 1) % wide) for i in range(1, wide, 2)]
    even_pairs = [(i, i + 1) for i in range(0, wide, 2)]
    odd_narrow = [(i, (i + 1) % narrow) for i in range(1, narrow, 2)]
    even_narrow = [(i, i + 1) for i in range(0, narrow, 2)]
    from_odd = exchange(outgoing[1], "wide", odd_pairs)
    from_even_n = exchange(outgoing[2], "narrow", even_narrow)
    from_odd_n = exchange(outgoing[3], "narrow", odd_narrow)
    from_even = exchange(outgoing[0], "wide", even_pairs)
    fine_ahead = call(
        fine_ahead_kernel,
        [rows_kept, fine_neighbors.T, fine_assign, edge_weights],
        [None, None, None, 0],
        [(fine_rows, width), weights[0], (8 * ahead, width), (coarse_rows, fine_rows)],
        [table((fine_rows // 2, 2 * width))],
        2 * 8 * ahead * fine_rows * width,
        "fine_ahead",
    )
    fine_mid, coarse_in, sender = call(
        functools.partial(fine_kernel, block=block),
        [parity, rows_kept, fine_neighbors.T]
        + [from_odd, from_even_n, from_odd_n, from_even]
        + list(fine_ahead)
        + params
        + [edge_weights],
        [smem] + [None] * 10 + [0, 0, 0, 0, 1],
        [(fine_rows, width), (coarse_rows, width), (coarse_rows, width)],
        [
            table(((fine_rows + 4 * halo) // 2, 2 * width)),
            table((2 * halo, 2 * width)),
            table((fine_rows, width)),
        ],
        2 * 8 * fine_rows * (fine_rows + 4 * halo) * width,
        "fine_level",
    )
    far_n = from_partner(sender, "narrow", 2)
    near_n = from_partner(sender, "narrow", 1)
    far_w = from_partner(sender, "wide", 2)
    near_w = from_partner(sender, "wide", 1)
    top_pad = -(-top_rows // 128) * 128
    *coarse_ahead, fine_hot, top_hot = call(
        coarse_ahead_kernel,
        [sender, coarse_neighbors.T, fine_assign, coarse_assign, edge_weights, node_weights],
        [None, None, None, None, 1, 1],
        weights + [(8 * coarse_rows, width), (fine_rows, coarse_rows), (fine_rows, top_pad)],
        [table((-(-coarse_rows // 256) * 128, 2 * width))],
        2 * 8 * coarse_rows * coarse_rows * width,
        "coarse_ahead",
    )
    coarse_mid, top_in, sender = call(
        coarse_kernel,
        [coarse_in, coarse_neighbors.T, coarse_assign, far_n, near_n, far_w, near_w]
        + list(coarse_ahead)
        + params
        + [edge_weights],
        [None] * 10 + [1, 1, 1, 1, 2],
        [(coarse_rows, width), (top_rows, width), (top_rows, width)],
        [table((-(-4 * coarse_rows // 256) * 128, 2 * width))],
        2 * 8 * coarse_rows * 4 * coarse_rows * width,
        "coarse_level",
    )
    wide_bits = wide.bit_length() - 1
    arrived = [from_partner(sender, "wide", 1 << bit) for bit in range(wide_bits)]
    arrived[3] = from_partner(arrived[2], "wide", 12)
    arrived[5] = from_partner(arrived[4], "wide", 48)
    arrived = [arrived[bit] for bit in (1, 0, 2, 4, 3, 5)]
    coarsest_ahead = call(
        functools.partial(coarsest_ahead_kernel, blank=(wide_bits + 1) * top_rows),
        [sender, coarsest_neighbors.T, fine_hot, fine_mid, coarse_mid]
        + [edge_weights, node_weights],
        [None] * 5 + [2, 2],
        weights + [(8 * top_pad, width), jax.ShapeDtypeStruct((fine_rows, width), F32)],
        [table((128, 2 * width))],
        2 * fine_rows * coarse_rows * width,
        "coarsest_ahead",
    )
    (result,) = call(
        coarsest_kernel,
        [top_in, coarsest_neighbors.T]
        + arrived
        + list(coarsest_ahead)
        + [top_hot]
        + params,
        [None] * 13 + [2, 2, 2, 2],
        [(fine_rows, width)],
        [table((-(-wide_bits * top_rows // 256) * 128, 2 * width))],
        2 * fine_rows * coarse_rows * width,
        "coarsest_level",
    )
    return result


def solution(mesh):
    rows = P(("wide", "narrow"), None)
    flat = P(("wide", "narrow"))
    in_specs = (rows, rows, P(("wide", "narrow"), None, None), rows, rows, flat, flat) + (P(),) * 4
    return jax.shard_map(
        on_device, mesh=mesh, in_specs=in_specs, out_specs=rows, check_vma=False
    )
```

```python
import functools

import jax
import jax.numpy as jnp
from jax import lax
from jax.experimental import pallas as pl
from jax.experimental.pallas import tpu as pltpu
from jax.sharding import PartitionSpec as P

F32 = jnp.float32
BF16 = jnp.bfloat16
I16 = jnp.int16
VMEM_BYTES = 24 * 1024 * 1024


def exchange(block, axis, pairs):
    route = [(i, j) for i, j in pairs] + [(j, i) for i, j in pairs]
    return lax.ppermute(block, axis, route)


def from_partner(block, axis, apart):
    count = lax.axis_size(axis)
    return lax.ppermute(block, axis, [(i, i ^ apart) for i in range(count)])


def dot(a, b):
    return jnp.dot(a, b, preferred_element_type=F32)


def one_hot(column, width):
    lanes = lax.broadcasted_iota(jnp.int32, (column.shape[0], width), 1)
    return (column == lanes).astype(BF16)


def centred_columns(matrix):
    wide = matrix.astype(F32)
    return wide - jnp.mean(wide, axis=-1, keepdims=True)


def block_diag(matrix):
    zero = jnp.zeros_like(matrix)
    return jnp.concatenate(
        [jnp.concatenate([matrix, zero], axis=1), jnp.concatenate([zero, matrix], axis=1)], axis=0
    )


def fill_table(table, pieces):
    half = table.shape[0]
    start = 0
    for piece in pieces:
        rows = piece.shape[0]
        cut = min(rows, max(0, half - start))
        if cut > 0:
            table[start : start + cut, 0:128] = piece[0:cut]
        if cut < rows:
            low = start + cut - half
            table[low : low + rows - cut, 128:256] = piece[cut:rows]
        start += rows
    if start < half:
        table[start:half, 0:128] = jnp.zeros((half - start, 128), BF16)
    gap = max(start - half, 0)
    if gap < half:
        table[gap:half, 128:256] = jnp.zeros((half - gap, 128), BF16)


def lane_broadcast(row):
    tiles = [
        jnp.broadcast_to(row[:, b : b + 128], (128, 128)).astype(I16).T
        for b in range(0, row.shape[1], 128)
    ]
    return jnp.concatenate(tiles, axis=0) if len(tiles) > 1 else tiles[0]


def one_hot_lanes(code, width):
    parts = []
    for start in range(0, width, 128):
        lanes = lax.broadcasted_iota(I16, code.shape, 1) + I16(start)
        parts.append(jnp.where(code == lanes, BF16(1), BF16(0)))
    return jnp.concatenate(parts, axis=1)


def spread_slots(nbr):
    return jnp.concatenate([lane_broadcast(nbr[k : k + 1]) for k in range(nbr.shape[0])], axis=0)


def picked_rows(code, table):
    half = table.shape[0]
    high = code >= I16(half)
    low = jnp.where(high, code - I16(half), code)
    got = dot(one_hot_lanes(low, half), table[...]).astype(BF16)
    return jnp.where(high, got[:, 128:256], got[:, 0:128])


def unit_rows(c):
    return c * lax.rsqrt(jnp.mean(c * c, axis=-1, keepdims=True) + 1e-5)


def edge_sums(x, nbr, table, first, partial, blank, mats, rows):
    w_recv, w_out2 = mats[:2]
    b_hid, b_out2, gain_e, empty = rows[:4]
    block = x.shape[0]
    slots = nbr.shape[0]
    receive = dot(x, w_recv) + b_hid
    code = spread_slots(nbr)
    sent = picked_rows(code - I16(first) if first else code, table)
    if partial is not None:
        sent = sent + partial
    sent = sent.astype(F32)
    hid = jnp.maximum(jnp.concatenate([receive] * slots, axis=0) + sent, 0.0).astype(BF16)
    hid = jnp.where(code < I16(blank), hid, BF16(0))
    split = slots // 2 * block
    c = dot(jnp.concatenate([hid[:split], hid[split:]], axis=1), w_out2) + b_out2
    m = unit_rows(c[:, 0:128]) + unit_rows(c[:, 128:256])
    total = m[0:block]
    for k in range(1, slots // 2):
        total = total + m[k * block : (k + 1) * block]
    missing = jnp.sum((nbr >= blank).astype(F32), axis=0, keepdims=True)
    missing = jnp.broadcast_to(missing, (8, block)).T[:, 0:1]
    return ((total - missing * empty) * gain_e).astype(BF16)


def node_step(x, summed, mats, rows):
    w_node, w_last = mats[2:]
    b_node, b_last, gain_n = rows[4:]
    upd = jnp.maximum(dot(jnp.concatenate([x, summed], axis=1), w_node) + b_node, 0.0).astype(BF16)
    return (x.astype(F32) + unit_rows(dot(upd, w_last) + b_last) * gain_n).astype(BF16)


def edge_weight(ew):
    return block_diag(centred_columns(ew[0, 2]).astype(BF16))


def last_weight(nw):
    return centred_columns(nw[0, 2]).astype(BF16)


def level_params(ew, nw, bias, gain, w_out2, w_last):
    w_node = jnp.concatenate([nw[0, 0], nw[0, 1]], axis=0)
    mats = (ew[0, 0], w_out2[...], w_node, w_last)
    b = bias[0]
    b_out = b[1:2] - jnp.mean(b[1:2])
    b_last = b[3:4] - jnp.mean(b[3:4])
    g = gain[0]
    b_pair = jnp.concatenate([b_out, b_out], axis=1)
    rows = (b[0:1], b_pair, g[0:1], unit_rows(b_out), b[2:3], b_last, g[1:2])
    return mats, rows


def membership(assign, groups):
    rows = assign.shape[1]
    group = lax.broadcasted_iota(I16, (groups, rows), 0)
    spread = jnp.broadcast_to(assign, (groups, rows)).astype(I16)
    return jnp.where(group == spread, BF16(1), BF16(0))


def listed_kernel(par_ref, send_ref, hot_ref, code_ref):
    lists = []
    for axis in range(2):
        odd = par_ref[axis] == 1
        up, down = send_ref[0, 2 * axis : 2 * axis + 1], send_ref[0, 2 * axis + 1 : 2 * axis + 2]
        lists += [jnp.where(odd, down, up), jnp.where(odd, up, down)]
    code = lane_broadcast(jnp.concatenate(lists, axis=1))
    code_ref[...] = code
    half = hot_ref.shape[1]
    hot_ref[...] = one_hot_lanes(jnp.where(code >= I16(half), code - I16(half), code), half)


def outgoing_kernel(x_ref, hot_ref, code_ref, *out_refs):
    x = x_ref[...]
    out_refs[4][...] = x
    half = x.shape[0] // 2
    pair = jnp.concatenate([x[:half], x[half:]], axis=1)
    got = dot(hot_ref[...], pair).astype(BF16)
    got = jnp.where(code_ref[...] >= I16(half), got[:, 128:256], got[:, 0:128])
    rows = out_refs[0].shape[0]
    for k, out in enumerate(out_refs[:4]):
        out[...] = got[k * rows : (k + 1) * rows]


def fine_ahead_kernel(
    x_ref, nbr_ref, assign_ref, ew, own_ref, edge_ref, part_ref, member_ref, table
):
    own = dot(x_ref[...], ew[0, 1]).astype(BF16)
    own_ref[...] = own
    edge_ref[...] = edge_weight(ew)
    fill_table(table, [own])
    part_ref[...] = picked_rows(spread_slots(nbr_ref[:, : part_ref.shape[0] // 8]), table)
    member_ref[...] = membership(assign_ref[...], member_ref.shape[0])


def fine_kernel(
    par_ref, x_ref, nbr_ref, h1, h2, h3, h0, own_ref, edge_ref, part_ref, member_ref,
    ew, nw, bias, gain, ew1,
    mid_ref, coarse_ref, sender_ref, table, near_table, sums, *, block
):
    x = x_ref[...]
    halo = []
    for axis, (first, second) in enumerate(((h0, h1), (h2, h3))):
        odd = par_ref[axis] == 1
        first, second = first[...], second[...]
        halo += [jnp.where(odd, first, second), jnp.where(odd, second, first)]
    halo = [dot(jnp.concatenate(halo, axis=0), ew[0, 1]).astype(BF16)]
    own = own_ref[...]
    fill_table(table, [own] + halo)
    fill_table(near_table, halo)
    mats, rows = level_params(ew, nw, bias, gain, edge_ref, last_weight(nw))
    rows_total = x_ref.shape[0]
    blank = rows_total + sum(piece.shape[0] for piece in halo)
    done = part_ref.shape[0] // 8
    sums[0:done] = edge_sums(
        x[0:done], nbr_ref[:, 0:done], near_table, rows_total, part_ref[...], blank, mats, rows
    )

    def step(j, carry):
        here = pl.ds(pl.multiple_of(j * block, block), block)
        nbr = nbr_ref[:, here]
        sums[here, :] = edge_sums(x_ref[here, :], nbr, table, 0, None, blank, mats, rows)
        return carry

    lax.fori_loop(done // block, rows_total // block, step, 0)
    mid = node_step(x, sums[...], mats, rows)
    mid_ref[...] = mid
    coarse = (dot(member_ref[...], mid) * 0.25).astype(BF16)
    coarse_ref[...] = coarse
    sender_ref[...] = dot(coarse, ew1[0, 1]).astype(BF16)


def coarse_ahead_kernel(
    sender_ref, nbr_ref, fine_assign, coarse_assign, ew, nw,
    edge_ref, last_ref, part_ref, fine_hot, top_hot, table
):
    hot = one_hot_lanes(lane_broadcast(fine_assign[...]), fine_hot.shape[1])
    fine_hot[...] = hot
    coarse_hot = one_hot_lanes(lane_broadcast(coarse_assign[...]), top_hot.shape[1])
    top_hot[...] = dot(hot, coarse_hot).astype(BF16)
    edge_ref[...] = edge_weight(ew)
    last_ref[...] = last_weight(nw)
    fill_table(table, [sender_ref])
    part_ref[...] = picked_rows(spread_slots(nbr_ref[...]), table)


def coarse_kernel(
    x_ref, nbr_ref, assign_ref, s4, s3, s2, s1, edge_ref, last_ref, part_ref,
    ew, nw, bias, gain, ew1,
    mid_ref, coarse_ref, sender_ref, table
):
    fill_table(table, [s1, s2, s3, s4])
    mats, rows = level_params(ew, nw, bias, gain, edge_ref, last_ref[...])
    x = x_ref[...]
    count = x.shape[0]
    sums = edge_sums(x, nbr_ref[...], table, count, part_ref[...], 5 * count, mats, rows)
    mid = node_step(x, sums, mats, rows)
    mid_ref[...] = mid
    coarse = (dot(membership(assign_ref[...], coarse_ref.shape[0]), mid) * 0.25).astype(BF16)
    coarse_ref[...] = coarse
    sender_ref[...] = dot(coarse, ew1[0, 1]).astype(BF16)


def padded_nbr(nbr_ref, blank):
    extra = -nbr_ref.shape[1] % 128
    return jnp.concatenate([nbr_ref[...], jnp.full((8, extra), blank, jnp.int32)], axis=1)


def coarsest_ahead_kernel(
    sender_ref, nbr_ref, fine_hot, fine_ref, coarse_ref, ew, nw,
    edge_ref, last_ref, part_ref, base_ref, table, *, blank
):
    edge_ref[...] = edge_weight(ew)
    last_ref[...] = last_weight(nw)
    fill_table(table, [sender_ref])
    part_ref[...] = picked_rows(spread_slots(padded_nbr(nbr_ref, blank)), table)
    base_ref[...] = fine_ref[...].astype(F32) + dot(fine_hot[...], coarse_ref[...])


def coarsest_kernel(
    x_ref, nbr_ref, s2, s1, s3, s5, s4, s6, edge_ref, last_ref, part_ref, base_ref, top_hot,
    ew, nw, bias, gain, out_hbm, table, stage, sems
):
    pieces = [s1, s2, s3, s4, s5, s6]
    fill_table(table, pieces)
    mats, rows = level_params(ew, nw, bias, gain, edge_ref, last_ref[...])
    count = x_ref.shape[0]
    blank = (len(pieces) + 1) * count
    x = jnp.concatenate([x_ref[...], jnp.zeros((-count % 128, 128), BF16)], axis=0)
    nbr = padded_nbr(nbr_ref, blank)
    sums = edge_sums(x, nbr, table, count, part_ref[...], blank, mats, rows)
    top = node_step(x, sums, mats, rows)
    parts = sems.shape[0]
    rows = stage.shape[0] // parts
    copies = []
    for k in range(parts):
        here = slice(k * rows, (k + 1) * rows)
        stage[here] = (base_ref[here] + dot(top_hot[here], top)).astype(BF16)
        copies.append(pltpu.make_async_copy(stage.at[here], out_hbm.at[here], sems.at[k]))
        copies[-1].start()
    for copy in copies:
        copy.wait()


def call(kernel, operands, specs, outs, scratch, flops, name, vmem_bytes=VMEM_BYTES, out_hbm=False):
    moved = sum(o.size * o.dtype.itemsize for o in operands)
    vmem = pl.BlockSpec(memory_space=pltpu.VMEM)

    def body(*refs):
        views = [
            ref.at[pl.ds(spec, 1)] if isinstance(spec, int) else ref for ref, spec in zip(refs, specs)
        ]
        kernel(*views, *refs[len(specs) :])

    return pl.pallas_call(
        body,
        in_specs=[vmem if spec is None or isinstance(spec, int) else spec for spec in specs],
        out_specs=[pl.BlockSpec(memory_space=pltpu.HBM) if out_hbm else vmem] * len(outs),
        out_shape=[o if hasattr(o, "dtype") else jax.ShapeDtypeStruct(o, BF16) for o in outs],
        scratch_shapes=scratch,
        compiler_params=pltpu.CompilerParams(vmem_limit_bytes=vmem_bytes),
        cost_estimate=pl.CostEstimate(flops=flops, bytes_accessed=moved, transcendentals=0),
        name=name,
    )(*operands)


def on_device(
    node_features,
    fine_neighbors,
    send_rows,
    coarse_neighbors,
    coarsest_neighbors,
    fine_assign,
    coarse_assign,
    edge_weights,
    node_weights,
    biases,
    gains,
):
    fine_rows, width = node_features.shape
    coarse_rows = coarse_neighbors.shape[0]
    top_rows = coarsest_neighbors.shape[0]
    halo = send_rows.shape[2]
    fine_assign = fine_assign.reshape(1, -1)
    coarse_assign = coarse_assign.reshape(1, -1)
    params = [edge_weights, node_weights, biases, gains]
    wide, narrow = lax.axis_size("wide"), lax.axis_size("narrow")
    parity = jnp.stack([lax.axis_index("wide") % 2, lax.axis_index("narrow") % 2])
    smem = pl.BlockSpec(memory_space=pltpu.SMEM)

    listed = call(
        listed_kernel,
        [parity, send_rows],
        [smem, None],
        [(4 * halo, fine_rows // 2), jax.ShapeDtypeStruct((4 * halo, width), I16)],
        [],
        8 * 4 * halo * fine_rows * width,
        "listed",
    )
    *outgoing, rows_kept = call(
        outgoing_kernel,
        [node_features] + list(listed),
        [None, None, None],
        [(halo, width)] * 4 + [(fine_rows, width)],
        [],
        8 * 2 * 4 * halo * fine_rows * width,
        "outgoing",
    )
    block = 512
    ahead = 1 * block
    table = functools.partial(pltpu.VMEM, dtype=BF16)
    weights = [(2 * width, 2 * width), (width, width)]
    odd_pairs = [(i, (i + 1) % wide) for i in range(1, wide, 2)]
    even_pairs = [(i, i + 1) for i in range(0, wide, 2)]
    odd_narrow = [(i, (i + 1) % narrow) for i in range(1, narrow, 2)]
    even_narrow = [(i, i + 1) for i in range(0, narrow, 2)]
    from_odd = exchange(outgoing[1], "wide", odd_pairs)
    from_even_n = exchange(outgoing[2], "narrow", even_narrow)
    from_odd_n = exchange(outgoing[3], "narrow", odd_narrow)
    from_even = exchange(outgoing[0], "wide", even_pairs)
    fine_ahead = call(
        fine_ahead_kernel,
        [rows_kept, fine_neighbors.T, fine_assign, edge_weights],
        [None, None, None, 0],
        [(fine_rows, width), weights[0], (8 * ahead, width), (coarse_rows, fine_rows)],
        [table((fine_rows // 2, 2 * width))],
        2 * 8 * ahead * fine_rows * width,
        "fine_ahead",
    )
    fine_mid, coarse_in, sender = call(
        functools.partial(fine_kernel, block=block),
        [parity, rows_kept, fine_neighbors.T]
        + [from_odd, from_even_n, from_odd_n, from_even]
        + list(fine_ahead)
        + params
        + [edge_weights],
        [smem] + [None] * 10 + [0, 0, 0, 0, 1],
        [(fine_rows, width), (coarse_rows, width), (coarse_rows, width)],
        [
            table(((fine_rows + 4 * halo) // 2, 2 * width)),
            table((2 * halo, 2 * width)),
            table((fine_rows, width)),
        ],
        2 * 8 * fine_rows * (fine_rows + 4 * halo) * width,
        "fine_level",
    )
    far_n = from_partner(sender, "narrow", 2)
    near_n = from_partner(sender, "narrow", 1)
    far_w = from_partner(sender, "wide", 2)
    near_w = from_partner(sender, "wide", 1)
    top_pad = -(-top_rows // 128) * 128
    *coarse_ahead, fine_hot, top_hot = call(
        coarse_ahead_kernel,
        [sender, coarse_neighbors.T, fine_assign, coarse_assign, edge_weights, node_weights],
        [None, None, None, None, 1, 1],
        weights + [(8 * coarse_rows, width), (fine_rows, coarse_rows), (fine_rows, top_pad)],
        [table((-(-coarse_rows // 256) * 128, 2 * width))],
        2 * 8 * coarse_rows * coarse_rows * width,
        "coarse_ahead",
    )
    coarse_mid, top_in, sender = call(
        coarse_kernel,
        [coarse_in, coarse_neighbors.T, coarse_assign, far_n, near_n, far_w, near_w]
        + list(coarse_ahead)
        + params
        + [edge_weights],
        [None] * 10 + [1, 1, 1, 1, 2],
        [(coarse_rows, width), (top_rows, width), (top_rows, width)],
        [table((-(-4 * coarse_rows // 256) * 128, 2 * width))],
        2 * 8 * coarse_rows * 4 * coarse_rows * width,
        "coarse_level",
    )
    wide_bits = wide.bit_length() - 1
    arrived = [from_partner(sender, "wide", 1 << bit) for bit in range(wide_bits)]
    arrived[3] = from_partner(arrived[2], "wide", 12)
    arrived[5] = from_partner(arrived[4], "wide", 48)
    arrived = [arrived[bit] for bit in (1, 0, 2, 4, 3, 5)]
    coarsest_ahead = call(
        functools.partial(coarsest_ahead_kernel, blank=(wide_bits + 1) * top_rows),
        [sender, coarsest_neighbors.T, fine_hot, fine_mid, coarse_mid]
        + [edge_weights, node_weights],
        [None] * 5 + [2, 2],
        weights + [(8 * top_pad, width), jax.ShapeDtypeStruct((fine_rows, width), F32)],
        [table((128, 2 * width))],
        2 * fine_rows * coarse_rows * width,
        "coarsest_ahead",
    )
    (result,) = call(
        coarsest_kernel,
        [top_in, coarsest_neighbors.T]
        + arrived
        + list(coarsest_ahead)
        + [top_hot]
        + params,
        [None] * 13 + [2, 2, 2, 2],
        [(fine_rows, width)],
        [
            table((-(-wide_bits * top_rows // 256) * 128, 2 * width)),
            table((fine_rows, width)),
            pltpu.SemaphoreType.DMA((3,)),
        ],
        2 * fine_rows * coarse_rows * width,
        "coarsest_level",
        out_hbm=True,
    )
    return result


def solution(mesh):
    rows = P(("wide", "narrow"), None)
    flat = P(("wide", "narrow"))
    in_specs = (rows, rows, P(("wide", "narrow"), None, None), rows, rows, flat, flat) + (P(),) * 4
    return jax.shard_map(
        on_device, mesh=mesh, in_specs=in_specs, out_specs=rows, check_vma=False
    )
```
